32 devices in a mesh: inline: 16 (over z, y, core), shot: 2 (over x).
Axes of the slice: x: 2, y: 2, z: 4, core: 2. Of those that a mesh axis runs over, the one named last changes fastest.
Arguments:
- source: bfloat16 [8, 512, 32, 256], P('shot', 'inline'), may hold values from -6 to 6
- receiver: bfloat16 [8, 512, 32, 256], P('shot', 'inline'), may hold values from -6 to 6
Outputs:
- offset_image: float32 [129, 512, 256], P(None, 'inline', 'shot')
The draws below stay inside these ranges and needn't reach their ends.
All inputs are finite; a program needn't handle non-finite values.
Results may differ from the reference program's by a relative error of at most 0.0003.
Values may be sent and summed in bfloat16 or wider, within the bound.
No kernel may reach another device: no remote copies, remote signals or barrier semaphores. Data moves between devices by JAX's collectives and lax.ppermute only.
A program may use at most 192 MiB of HBM per device.

```python
import jax
import jax.numpy as jnp
from jax import lax

HLAG = 64
NY = 256
NT = 32
CX = 32
NX = 512
SHOTS = 8


def spiked(array, key, source, target, parts, factor):
    owner, partner = [(jnp.arange(array.shape[position]) // (array.shape[position] // parts)).reshape([-1 if axis == position else 1 for axis in range(array.ndim)]) for position in (source, target)]
    chosen = jax.random.permutation(key, parts)[partner]
    strong = (owner == chosen) | (owner == (partner + parts // 2) % parts)
    return jnp.where(strong, factor * array, array)


def levels(own_key, shape, pieces, least, top_value):
    def one(dim, blocks):
        heights = jax.random.uniform(jax.random.fold_in(jax.random.fold_in(own_key, 6), dim), (blocks,), jnp.float32, least / len(pieces), top_value / len(pieces))
        return jnp.repeat(jnp.exp(heights), shape[dim] // blocks).reshape((-1,) + (1,) * (len(shape) - dim - 1))

    loudness = one(*pieces[0])
    for cut in pieces[1:]:
        loudness = loudness * one(*cut)
    return loudness


def centred(stream_key, dims, deviation, bound, shards=(), held_as=jnp.bfloat16):
    loudness = levels(stream_key, dims, shards, -0.22, 0.18) if shards else 1.0
    values = jax.random.normal(stream_key, dims, jnp.float32) * deviation * loudness
    return jnp.minimum(jnp.maximum(values, -bound), bound).astype(held_as)


def bell_draw_with(own_key, dims, spread, limit, cuts, heavy, kind=jnp.bfloat16):
    entries = spread * jax.random.normal(own_key, dims, jnp.float32)
    if cuts:
        entries = entries * levels(own_key, dims, cuts, -0.22, 0.18)
    return jnp.clip(spiked(entries, jax.random.fold_in(own_key, 3), *heavy), -limit, limit).astype(kind)


def setup_inputs(seed: int = 0) -> dict:
    streams_of = jax.random.split(jax.random.key(seed), 3)
    return {
        "source": centred(streams_of[0], (SHOTS, NX, NT, NY), 1.0, 6.0, ((0, 2), (1, 16))),
        "receiver": bell_draw_with(streams_of[1], (SHOTS, NX, NT, NY), 1.0, 6.0, ((0, 2), (1, 16)), (0, 3, 2, 2.0)),
    }


def band_of(product, width, lags):
    rows = product.shape[1]
    flat = product.reshape(product.shape[0], rows * width)
    flat = jnp.pad(flat, ((0, 0), (0, rows)))
    skewed = flat.reshape(product.shape[0], rows, width + 1)[:, :, :lags]
    return jnp.transpose(skewed, (2, 1, 0))


def reference(source, receiver):
    padded = jnp.pad(receiver, ((0, 0), (HLAG, HLAG), (0, 0), (0, 0)))
    width = CX + 2 * HLAG

    def one_block(block):
        start = (block * CX).astype(jnp.int32)
        left = lax.dynamic_slice_in_dim(source, start, CX, 1).astype(jnp.float32)
        right = lax.dynamic_slice_in_dim(padded, start, width, 1).astype(jnp.float32)
        product = jnp.einsum("sity,szty->yiz", left, right, precision=lax.Precision.HIGHEST)
        return band_of(product, width, 2 * HLAG + 1)

    blocks = lax.map(one_block, jnp.arange(NX // CX, dtype=jnp.int32))
    image = jnp.transpose(blocks, (1, 0, 2, 3)).reshape(2 * HLAG + 1, NX, NY)
    return image * (1.0 / (NT * SHOTS) ** 0.5)
```

```python
import functools

import jax
import jax.numpy as jnp
from jax import lax
from jax.experimental import pallas as pl
from jax.experimental.pallas import tpu as pltpu
from jax.sharding import PartitionSpec as P

LANES = 128
ROWS = 16
VMEM_BYTES = 48 * 1024 * 1024


def shifted(value, axis, steps):
    count = lax.axis_size(axis)
    initial, last = (max(0, -steps), min(count, count - steps))
    return lax.ppermute(value, axis, [(source, source + steps) for source in range(initial, last)])


def band_rows(product, width, lags):
    rows = product.shape[0]
    cross = product.shape[2]
    flat = product.reshape(rows * width, cross)
    flat = jnp.pad(flat, ((0, rows), (0, 0)))
    skewed = flat.reshape(rows, width + 1, cross)[:, :lags, :]
    return jnp.transpose(skewed, (1, 0, 2))


def plain(source, receiver, scale):
    source, receiver = (
        lax.all_to_all(value, "shot", split_axis=3, concat_axis=0, tiled=True) for value in (source, receiver)
    )
    cells = source.shape[1]
    slabs = [receiver if step == 0 else shifted(receiver, "inline", -step) for step in (-2, -1, 0, 1, 2)]
    width = 5 * cells
    product = jnp.einsum(
        "sity,szty->izy", source, jnp.concatenate(slabs, axis=1), preferred_element_type=jnp.float32
    )
    return band_rows(product, width, 4 * cells + 1) * scale


def turn_body(half_ref, raw_ref, turned_ref, rows_ref):
    shots, cells, times, cross = raw_ref.shape
    for cell in range(cells):
        tile = raw_ref[:, cell].reshape(shots * times, cross).astype(jnp.float32)
        rows_ref[pl.ds(cell, cross, stride=cells), :] = tile.T
    turned_ref[...] = rows_ref[...].reshape(turned_ref.shape).astype(turned_ref.dtype)


def turn(raw, half):
    shots, cells, times, _ = raw.shape
    depth = shots * times
    return pl.pallas_call(
        turn_body,
        grid_spec=pltpu.PrefetchScalarGridSpec(
            num_scalar_prefetch=1,
            grid=(cells // ROWS,),
            in_specs=[pl.BlockSpec((shots, ROWS, times, LANES), lambda step, half: (0, step, 0, half[0]))],
            out_specs=pl.BlockSpec((LANES, ROWS, depth), lambda step, half: (0, step, 0)),
            scratch_shapes=[pltpu.VMEM((LANES * ROWS, depth), jnp.float32)],
        ),
        out_shape=jax.ShapeDtypeStruct((LANES, cells, depth), raw.dtype),
        compiler_params=pltpu.CompilerParams(vmem_limit_bytes=VMEM_BYTES),
        cost_estimate=pl.CostEstimate(flops=0, bytes_accessed=raw.size * 2, transcendentals=0),
        name="turn",
    )(half, raw)


def image_body(scale, cells, where_ref, *refs):
    sources, slots, image_ref = (refs[:2], [refs[2 + 2 * j : 4 + 2 * j] for j in range(5)], refs[12])
    wide_ref, narrow_ref, skewed_ref, sem = refs[13:]
    block = sources[0].shape[0]
    step = pl.program_id(0)

    def rows_of(pair, cross):
        return jnp.concatenate([part[cross] for part in pair], axis=1)

    dims = (((1,), (1,)), ((), ()))
    for cross in range(block):
        left = rows_of(sources, cross)
        right = [rows_of(pair, cross) for pair in slots]
        place = pl.ds(pl.multiple_of((step * block + cross) * cells, cells), cells)
        wide_ref[place, :] = lax.dot_general(
            left, jnp.concatenate(right[:4], axis=0), dims, preferred_element_type=jnp.float32
        )
        narrow_ref[place, :cells] = lax.dot_general(left, right[4], dims, preferred_element_type=jnp.float32)

    @pl.when(step == pl.num_programs(0) - 1)
    def _():
        for cell in range(cells):
            every = pl.ds(cell, LANES, stride=cells)
            turned = [wide_ref[every, :].T, narrow_ref[every, :].T[:cells]]
            pieces = [turned[0][cells * j : cells * (j + 1)] for j in range(4)] + [turned[1]]
            for j, piece in enumerate(pieces):
                lag = (where_ref[j] + 3) * cells - cell
                skewed_ref[pl.ds(lag * cells + cell, cells, stride=cells), :] = piece * scale
        copy = pltpu.make_async_copy(
            skewed_ref.at[pl.ds(cells * cells, image_ref.shape[0])], image_ref, sem
        )
        copy.start()
        copy.wait()


def image(scale, where, sources, slots):
    _, cells, depth = sources[0].shape
    lags = 4 * cells + 1
    block = 16
    spec = pl.BlockSpec((block, cells, depth), lambda step, where: (step, 0, 0))
    flat = [part for pair in (sources, *slots) for part in pair]
    return pl.pallas_call(
        functools.partial(image_body, scale, cells),
        grid_spec=pltpu.PrefetchScalarGridSpec(
            num_scalar_prefetch=1,
            grid=(LANES // block,),
            in_specs=[spec] * len(flat),
            out_specs=pl.BlockSpec(memory_space=pl.ANY),
            scratch_shapes=[
                pltpu.VMEM((LANES * cells, 4 * cells), jnp.float32),
                pltpu.VMEM((LANES * cells, LANES), jnp.float32),
                pltpu.VMEM(((lags + 2 * cells) * cells, LANES), jnp.float32),
                pltpu.SemaphoreType.DMA(()),
            ],
        ),
        out_shape=jax.ShapeDtypeStruct((lags * cells, LANES), jnp.float32),
        compiler_params=pltpu.CompilerParams(vmem_limit_bytes=VMEM_BYTES),
        name="image",
    )(where, *flat).reshape(lags, cells, LANES)


def routed(source, receiver, scale):
    count = lax.axis_size("inline")
    own = lax.axis_index("inline")
    core, odd = own % 2, own // 2 % 2
    half = lax.axis_index("shot")

    def across(value):
        return lax.ppermute(value, "shot", [(0, 1), (1, 0)])

    def along_y(value):
        return lax.ppermute(value, "inline", [(index, index ^ 2) for index in range(count)])

    def along_z(value):
        pairs = [(index, index + (4 if index // 2 % 2 == 0 else -4)) for index in range(count)]
        return lax.ppermute(value, "inline", [pair for pair in pairs if 0 <= pair[1] < count])

    def to_core(value):
        return lax.ppermute(value, "inline", [(index, index ^ 1) for index in range(count)])

    here, there = (jnp.full((1,), index, jnp.int32) for index in (half, 1 - half))
    sent = turn(receiver, there)
    kept = turn(receiver, here)
    slots = []
    for part in (kept, across(sent)):
        from_y = along_y(part)
        from_z = along_z(from_y)
        twin = to_core(part)
        shared = jnp.where(core == odd, to_core(from_z), to_core(from_y))
        slots.append((from_y, from_z, part, twin, shared))
    sources = (turn(source, here), across(turn(source, there)))
    where = jnp.stack([2 - 4 * odd, 4 * odd - 2, 0 * odd, 1 - 2 * core, 2 * core - 1]).astype(jnp.int32)
    return image(scale, where, sources, list(zip(*slots)))


def on_device(source, receiver):
    shots, cells, times, cross = source.shape
    groups, count = lax.axis_size("shot"), lax.axis_size("inline")
    scale = 1.0 / (times * shots * groups) ** 0.5
    fits = (
        groups == 2
        and count % 4 == 0
        and cross == 2 * LANES
        and shots * times == LANES
        and 4 * cells == LANES
        and times % ROWS == 0
    )
    return routed(source, receiver, scale) if fits else plain(source, receiver, scale)


def solution(mesh):
    placed = (P("shot", "inline", None, None), P("shot", "inline", None, None))
    return jax.shard_map(
        on_device, mesh=mesh, in_specs=placed, out_specs=P(None, "inline", "shot"), check_vma=False
    )
```

```python
import functools

import jax
import jax.numpy as jnp
from jax import lax
from jax.experimental import pallas as pl
from jax.experimental.pallas import tpu as pltpu
from jax.sharding import PartitionSpec as P

LANES = 128
ROWS = 16
VMEM_BYTES = 20 * 1024 * 1024
TOP_BYTES = 60 * 1024 * 1024


def shifted(value, axis, steps):
    count = lax.axis_size(axis)
    initial, last = (max(0, -steps), min(count, count - steps))
    return lax.ppermute(value, axis, [(source, source + steps) for source in range(initial, last)])


def band_rows(product, width, lags):
    rows = product.shape[0]
    cross = product.shape[2]
    flat = product.reshape(rows * width, cross)
    flat = jnp.pad(flat, ((0, rows), (0, 0)))
    skewed = flat.reshape(rows, width + 1, cross)[:, :lags, :]
    return jnp.transpose(skewed, (1, 0, 2))


def plain(source, receiver, scale):
    source, receiver = (
        lax.all_to_all(value, "shot", split_axis=3, concat_axis=0, tiled=True) for value in (source, receiver)
    )
    cells = source.shape[1]
    slabs = [receiver if step == 0 else shifted(receiver, "inline", -step) for step in (-2, -1, 0, 1, 2)]
    width = 5 * cells
    product = jnp.einsum(
        "sity,szty->izy", source, jnp.concatenate(slabs, axis=1), preferred_element_type=jnp.float32
    )
    return band_rows(product, width, 4 * cells + 1) * scale


def turn_body(half_ref, raw_ref, *refs):
    *turned_refs, rows_ref = refs
    shots, cells, times, cross = raw_ref.shape
    for cell in range(cells):
        tile = raw_ref[:, cell].reshape(shots * times, cross).astype(jnp.float32)
        rows_ref[pl.ds(cell, cross, stride=cells), :] = tile.T
    share = cross // len(turned_refs)
    for part, turned_ref in enumerate(turned_refs):
        rows = rows_ref[pl.ds(part * share * cells, share * cells), :]
        turned_ref[...] = rows.reshape(turned_ref.shape).astype(turned_ref.dtype)


def turn(raw, half, parts, vmem, after=None):
    shots, cells, times, _ = raw.shape
    depth = shots * times
    extra = [] if after is None else [after]

    def body(half_ref, raw_ref, *refs):
        turn_body(half_ref, raw_ref, *refs[len(extra) :])

    return pl.pallas_call(
        body,
        grid_spec=pltpu.PrefetchScalarGridSpec(
            num_scalar_prefetch=1,
            grid=(cells // ROWS,),
            in_specs=[pl.BlockSpec((shots, ROWS, times, LANES), lambda step, half: (0, step, 0, half[0]))]
            + [pl.BlockSpec(memory_space=pl.ANY)] * len(extra),
            out_specs=[pl.BlockSpec((LANES // parts, ROWS, depth), lambda step, half: (0, step, 0))] * parts,
            scratch_shapes=[pltpu.VMEM((LANES * ROWS, depth), jnp.float32)],
        ),
        out_shape=[jax.ShapeDtypeStruct((LANES // parts, cells, depth), raw.dtype)] * parts,
        compiler_params=pltpu.CompilerParams(vmem_limit_bytes=vmem),
        cost_estimate=pl.CostEstimate(flops=0, bytes_accessed=raw.size * 2, transcendentals=0),
        name="turn",
    )(half, raw, *extra)


DIMS = (((1,), (1,)), ((), ()))


def choose(flag_ref, first, second, chosen):
    @pl.when(flag_ref[SLOTS] == 1)
    def _():
        for to, source in zip(chosen, first):
            to[...] = source[...]

    @pl.when(flag_ref[SLOTS] == 0)
    def _():
        for to, source in zip(chosen, second):
            to[...] = source[...]


def multiply(source_ref, slots, store):
    parts, block = source_ref.shape[:2]
    for part in range(parts):
        for cross in range(block):
            right = [slab[part][cross] for slab in slots]
            right = jnp.concatenate(right, axis=0) if len(right) > 1 else right[0]
            store(part, cross, lax.dot_general(source_ref[part, cross], right, DIMS, preferred_element_type=jnp.float32))


def spread(scale, cells, products_ref, skewed_ref, where_ref, slots):
    for cell in range(cells):
        turned = products_ref[pl.ds(cell, LANES, stride=cells), :].T * scale
        for place, slot in enumerate(slots):
            lag = (where_ref[slot] + 3) * cells - cell
            skewed_ref[pl.ds(lag * cells + cell, cells, stride=cells), :] = turned[cells * place : cells * (place + 1)]


def first_body(cells, where_ref, source_ref, *refs):
    ins, (wide_ref, late_ref), chosen = refs[:12], refs[12:14], refs[14:]
    slots = [ins[2 * j : 2 * j + 2] for j in range(6)]
    choose(where_ref, slots[4], slots[5], chosen)

    def store_wide(part, cross, value):
        wide_ref[part, pl.ds(cross * cells, cells), : 3 * cells] = value

    def store_late(part, cross, value):
        late_ref[part, pl.ds(cross * cells, cells), : 2 * cells] = value

    multiply(source_ref, slots[:3], store_wide)
    multiply(source_ref, [slots[3], chosen], store_late)


def specs_of(block, cells, depth):
    source = pl.BlockSpec((2, block, cells, depth), lambda step, where: (0, step, 0, 0))
    slab = pl.BlockSpec((block, cells, depth), lambda step, where: (step, 0, 0))
    products = pl.BlockSpec((2, block * cells, LANES), lambda step, where: (0, step, 0))
    return source, slab, products


BLOCK = 8
SLOTS = 5


def first(where, source, slots):
    _, half, cells, depth = source.shape
    source_spec, slab, products = specs_of(BLOCK, cells, depth)
    return pl.pallas_call(
        functools.partial(first_body, cells),
        grid_spec=pltpu.PrefetchScalarGridSpec(
            num_scalar_prefetch=1,
            grid=(half // BLOCK,),
            in_specs=[source_spec] + [slab] * 12,
            out_specs=[products] * 2,
            scratch_shapes=[pltpu.VMEM((BLOCK, cells, depth), source.dtype)] * 2,
        ),
        out_shape=[jax.ShapeDtypeStruct((2, half * cells, LANES), jnp.float32)] * 2,
        compiler_params=pltpu.CompilerParams(vmem_limit_bytes=VMEM_BYTES),
        name="first",
    )(where, source, *slots)


def adder(cells, step, half_rows, products_ref, total_ref, width):
    def store(part, cross, value):
        rows = pl.ds(cross * cells, cells)
        place = pl.multiple_of(part * half_rows + (step * BLOCK + cross) * cells, cells)
        total_ref[pl.ds(place, cells), :width] = value + products_ref[part, rows, :width]

    return store


def second_body(scale, cells, where_ref, source_ref, *refs):
    ins, products_ref, skewed_out, total_ref, skewed_ref, sem = refs[:6], *refs[6:]
    step = pl.program_id(0)
    slots = [ins[2 * j : 2 * j + 2] for j in range(3)]
    multiply(source_ref, slots, adder(cells, step, LANES // 2 * cells, products_ref, total_ref, 3 * cells))

    @pl.when(step == pl.num_programs(0) - 1)
    def _():
        spread(scale, cells, total_ref, skewed_ref, where_ref, (0, 1, 2))
        copy = pltpu.make_async_copy(skewed_ref, skewed_out, sem)
        copy.start()
        copy.wait()


def second(scale, where, source, slots, products):
    _, half, cells, depth = source.shape
    source_spec, slab, products_spec = specs_of(BLOCK, cells, depth)
    rows = (4 * cells + 1 + 2 * cells) * cells
    return pl.pallas_call(
        functools.partial(second_body, scale, cells),
        grid_spec=pltpu.PrefetchScalarGridSpec(
            num_scalar_prefetch=1,
            grid=(half // BLOCK,),
            in_specs=[source_spec] + [slab] * 6 + [products_spec],
            out_specs=pl.BlockSpec(memory_space=pl.ANY),
            scratch_shapes=[
                pltpu.VMEM((2 * half * cells, LANES), jnp.float32),
                pltpu.VMEM((rows, LANES), jnp.float32),
                pltpu.SemaphoreType.DMA(()),
            ],
        ),
        out_shape=jax.ShapeDtypeStruct((rows, LANES), jnp.float32),
        compiler_params=pltpu.CompilerParams(vmem_limit_bytes=VMEM_BYTES),
        name="second",
    )(where, source, *slots, products)


def third_body(scale, cells, where_ref, source_ref, *refs):
    ins, (products_ref, skewed_in, image_ref), (total_ref, skewed_ref, in_sem, out_sem) = refs[:6], refs[6:9], refs[9:13]
    chosen = refs[13:]
    step = pl.program_id(0)
    slots = [ins[2 * j : 2 * j + 2] for j in range(3)]
    load = pltpu.make_async_copy(skewed_in, skewed_ref, in_sem)

    @pl.when(step == 0)
    def _():
        load.start()

    choose(where_ref, slots[1], slots[2], chosen)
    multiply(
        source_ref, [slots[0], chosen], adder(cells, step, LANES // 2 * cells, products_ref, total_ref, 2 * cells)
    )

    @pl.when(step == pl.num_programs(0) - 1)
    def _():
        load.wait()
        spread(scale, cells, total_ref, skewed_ref, where_ref, (3, 4))
        copy = pltpu.make_async_copy(skewed_ref.at[pl.ds(cells * cells, image_ref.shape[0])], image_ref, out_sem)
        copy.start()
        copy.wait()


def third(scale, where, source, slots, products, skewed):
    _, half, cells, depth = source.shape
    source_spec, slab, products_spec = specs_of(BLOCK, cells, depth)
    lags = 4 * cells + 1
    return pl.pallas_call(
        functools.partial(third_body, scale, cells),
        grid_spec=pltpu.PrefetchScalarGridSpec(
            num_scalar_prefetch=1,
            grid=(half // BLOCK,),
            in_specs=[source_spec] + [slab] * 6 + [products_spec, pl.BlockSpec(memory_space=pl.ANY)],
            out_specs=pl.BlockSpec(memory_space=pl.ANY),
            scratch_shapes=[
                pltpu.VMEM((2 * half * cells, LANES), jnp.float32),
                pltpu.VMEM(skewed.shape, jnp.float32),
                pltpu.SemaphoreType.DMA(()),
                pltpu.SemaphoreType.DMA(()),
            ]
            + [pltpu.VMEM((BLOCK, cells, depth), source.dtype)] * 2,
        ),
        out_shape=jax.ShapeDtypeStruct((lags * cells, LANES), jnp.float32),
        compiler_params=pltpu.CompilerParams(vmem_limit_bytes=VMEM_BYTES),
        name="third",
    )(where, source, *slots, products, skewed).reshape(lags, cells, LANES)


def routed(source, receiver, scale):
    count = lax.axis_size("inline")
    own = lax.axis_index("inline")
    core, odd = own & 1, (own >> 1) & 1
    half = lax.axis_index("shot")

    def across(value):
        return lax.ppermute(value, "shot", [(0, 1), (1, 0)])

    def along_y(value):
        return lax.ppermute(value, "inline", [(index, index ^ 2) for index in range(count)])

    def along_z(value):
        pairs = [(index, index + (4 if index // 2 % 2 == 0 else -4)) for index in range(count)]
        return lax.ppermute(value, "inline", [pair for pair in pairs if 0 <= pair[1] < count])

    def to_core(value):
        return lax.ppermute(value, "inline", [(index, index ^ 1) for index in range(count)])

    here, there = (jnp.full((1,), index, jnp.int32) for index in (half, 1 - half))
    kept = turn(receiver, here, 2, TOP_BYTES)
    sent = turn(receiver, there, 2, VMEM_BYTES, kept[0])
    moved = [across(part) for part in sent]
    near = turn(source, here, 1, VMEM_BYTES, sent[0])[0]
    far = across(turn(source, there, 1, VMEM_BYTES, moved[1])[0])
    sources = [value.reshape(2, LANES // 2, *value.shape[1:]) for value in (near, far)]
    groups = []
    for parts in (kept, moved):
        from_y = [along_y(part) for part in parts]
        from_z = [along_z(part) for part in from_y]
        twin = [to_core(part) for part in parts]
        shared_y = [to_core(part) for part in from_y]
        shared_z = [to_core(part) for part in from_z]
        groups.append((*from_y, *parts, *twin, *from_z, *shared_y, *shared_z))
    where = jnp.stack(
        [2 - 4 * odd, 0 * odd, 1 - 2 * core, 4 * odd - 2, 2 * core - 1, core ^ odd]
    ).astype(jnp.int32)
    wide, late = first(where, sources[0], groups[0])
    skewed = second(scale, where, sources[1], groups[1][:6], wide)
    return third(scale, where, sources[1], groups[1][6:], late, skewed)


def on_device(source, receiver):
    shots, cells, times, cross = source.shape
    groups, count = lax.axis_size("shot"), lax.axis_size("inline")
    scale = 1.0 / (times * shots * groups) ** 0.5
    fits = (
        groups == 2
        and count % 4 == 0
        and cross == 2 * LANES
        and shots * times == LANES
        and 4 * cells == LANES
        and times % ROWS == 0
    )
    return routed(source, receiver, scale) if fits else plain(source, receiver, scale)


def solution(mesh):
    placed = (P("shot", "inline", None, None), P("shot", "inline", None, None))
    return jax.shard_map(
        on_device, mesh=mesh, in_specs=placed, out_specs=P(None, "inline", "shot"), check_vma=False
    )
```

```python
import functools

import jax
import jax.numpy as jnp
from jax import lax
from jax.experimental import pallas as pl
from jax.experimental.pallas import tpu as pltpu
from jax.sharding import PartitionSpec as P

LANES = 128
ROWS = 16
VMEM_BYTES = 16 * 1024 * 1024


def shifted(value, axis, steps):
    count = lax.axis_size(axis)
    initial, last = (max(0, -steps), min(count, count - steps))
    return lax.ppermute(value, axis, [(source, source + steps) for source in range(initial, last)])


def band_rows(product, width, lags):
    rows = product.shape[0]
    cross = product.shape[2]
    flat = product.reshape(rows * width, cross)
    flat = jnp.pad(flat, ((0, rows), (0, 0)))
    skewed = flat.reshape(rows, width + 1, cross)[:, :lags, :]
    return jnp.transpose(skewed, (1, 0, 2))


def plain(source, receiver, scale):
    source, receiver = (
        lax.all_to_all(value, "shot", split_axis=3, concat_axis=0, tiled=True) for value in (source, receiver)
    )
    cells = source.shape[1]
    slabs = [receiver if step == 0 else shifted(receiver, "inline", -step) for step in (-2, -1, 0, 1, 2)]
    width = 5 * cells
    product = jnp.einsum(
        "sity,szty->izy", source, jnp.concatenate(slabs, axis=1), preferred_element_type=jnp.float32
    )
    return band_rows(product, width, 4 * cells + 1) * scale


def turn_body(which_ref, raw_ref, *refs):
    own_ref, other_ref, rows_ref = refs[-3:]
    shots, cells, times, cross = raw_ref.shape
    for cell in range(cells):
        tile = raw_ref[:, cell].reshape(shots * times, cross).astype(jnp.float32)
        rows_ref[pl.ds(cell, cross, stride=cells), :] = tile.T
    share = cross // 2 * cells
    for turned_ref, part in ((own_ref, which_ref[1]), (other_ref, 1 - which_ref[1])):
        rows = rows_ref[pl.ds(pl.multiple_of(part * share, share), share), :]
        turned_ref[...] = rows.reshape(turned_ref.shape).astype(turned_ref.dtype)


def turn(raw, half, core):
    shots, cells, times, _ = raw.shape
    depth = shots * times
    share = LANES // 2
    return pl.pallas_call(
        turn_body,
        grid_spec=pltpu.PrefetchScalarGridSpec(
            num_scalar_prefetch=1,
            grid=(cells // ROWS,),
            in_specs=[pl.BlockSpec((shots, ROWS, times, LANES), lambda step, which: (0, step, 0, which[0]))],
            out_specs=[pl.BlockSpec((share, ROWS, depth), lambda step, which: (0, step, 0))] * 2,
            scratch_shapes=[pltpu.VMEM((LANES * ROWS, depth), jnp.float32)],
        ),
        out_shape=[jax.ShapeDtypeStruct((share, cells, depth), raw.dtype)] * 2,
        compiler_params=pltpu.CompilerParams(vmem_limit_bytes=VMEM_BYTES),
        cost_estimate=pl.CostEstimate(flops=0, bytes_accessed=raw.size * 2, transcendentals=0),
        name="turn",
    )(jnp.stack([half, core]).astype(jnp.int32), raw)


DIMS = (((1,), (1,)), ((), ()))
BLOCK = 16


def multiply_body(slabs, core_ref, *refs):
    sources, pieces, rest = refs[:2], refs[2 : 2 + slabs], refs[2 + slabs :]
    right_ref = rest[-1]
    groups = (slabs * sources[0].shape[1] + LANES - 1) // LANES
    kept, sent = rest[-1 - 2 * groups : -1 - groups], rest[-1 - groups : -1]
    before = rest[: -1 - 2 * groups]
    block, cells, _ = sources[0].shape
    for place, piece in enumerate(pieces):
        side, other = divmod(place, 2)
        right_ref[2 * side + (core_ref[0] if other == 0 else 1 - core_ref[0])] = piece[...]
    for cross in range(block):
        left = jnp.concatenate([source[cross] for source in sources], axis=0)
        rows = pl.ds(cross * cells, cells)
        for group in range(groups):
            members = range(group * LANES // cells, min(slabs, (group + 1) * LANES // cells))
            right = jnp.concatenate([right_ref[slab, cross] for slab in members], axis=0)
            width = len(members) * cells
            value = lax.dot_general(left, right, DIMS, preferred_element_type=jnp.float32)
            for out, part in ((kept[group], value[:cells]), (sent[group], value[cells:])):
                if before:
                    part = part + before[group if out is kept[group] else groups + group][rows, :width]
                out[rows, :width] = part


def multiply(core, sources, pieces, before=()):
    share, cells, depth = sources[0].shape
    slabs = len(pieces)
    groups = -(-slabs * cells // LANES)
    slab = pl.BlockSpec((BLOCK, cells, depth), lambda step, core: (step, 0, 0))
    products = pl.BlockSpec((BLOCK * cells, LANES), lambda step, core: (step, 0))
    flops = 2 * share * 2 * cells * slabs * cells * depth
    return pl.pallas_call(
        functools.partial(multiply_body, slabs),
        grid_spec=pltpu.PrefetchScalarGridSpec(
            num_scalar_prefetch=1,
            grid=(share // BLOCK,),
            in_specs=[slab] * (2 + slabs) + [products] * len(before),
            out_specs=[products] * (2 * groups),
            scratch_shapes=[pltpu.VMEM((slabs, BLOCK, cells, depth), sources[0].dtype)],
        ),
        out_shape=[jax.ShapeDtypeStruct((share * cells, LANES), jnp.float32)] * (2 * groups),
        compiler_params=pltpu.CompilerParams(vmem_limit_bytes=VMEM_BYTES),
        cost_estimate=pl.CostEstimate(flops=flops, bytes_accessed=4 << 20, transcendentals=0),
        name="multiply",
    )(core.reshape(1), *sources, *pieces, *before)


def spread_body(scale, cells, where_ref, *refs):
    products, image_ref, skewed_ref, sem = refs[:4], *refs[4:]
    core = where_ref[6]
    for cell in range(cells):
        for group, count in ((0, 4), (1, 2)):
            kept, came = (ref[pl.ds(cell, LANES // 2, stride=cells), :] for ref in products[2 * group : 2 * group + 2])
            low = jnp.where(core == 0, kept, came)
            high = jnp.where(core == 0, came, kept)
            turned = jnp.concatenate([low, high], axis=0).T * scale
            for place in range(count):
                lag = (where_ref[4 * group + place] + 4) * cells - cell
                skewed_ref[pl.ds(lag * cells + cell, cells, stride=cells), :] = turned[
                    cells * place : cells * (place + 1)
                ]
    copy = pltpu.make_async_copy(skewed_ref.at[pl.ds(2 * cells * cells, image_ref.shape[0])], image_ref, sem)
    copy.start()
    copy.wait()


def spread(scale, cells, where, products):
    lags = 4 * cells + 1
    return pl.pallas_call(
        functools.partial(spread_body, scale, cells),
        grid_spec=pltpu.PrefetchScalarGridSpec(
            num_scalar_prefetch=1,
            grid=(1,),
            in_specs=[pl.BlockSpec(products[0].shape, lambda step, where: (0, 0))] * 4,
            out_specs=pl.BlockSpec(memory_space=pl.ANY),
            scratch_shapes=[
                pltpu.VMEM(((lags + 4 * cells) * cells, LANES), jnp.float32),
                pltpu.SemaphoreType.DMA(()),
            ],
        ),
        out_shape=jax.ShapeDtypeStruct((lags * cells, LANES), jnp.float32),
        compiler_params=pltpu.CompilerParams(vmem_limit_bytes=VMEM_BYTES),
        name="spread",
    )(where, *products).reshape(lags, cells, LANES)


def routed(source, receiver, scale):
    count = lax.axis_size("inline")
    cells = source.shape[1]
    own = lax.axis_index("inline")
    core, odd = own & 1, (own >> 1) & 1
    half = lax.axis_index("shot")

    def across(value):
        return lax.ppermute(value, "shot", [(0, 1), (1, 0)])

    def along_y(value):
        return lax.ppermute(value, "inline", [(index, index ^ 2) for index in range(count)])

    def along_z(value):
        pairs = [(index, index + (4 if index // 2 % 2 == 0 else -4)) for index in range(count)]
        return lax.ppermute(value, "inline", [pair for pair in pairs if 0 <= pair[1] < count])

    def to_core(value):
        return lax.ppermute(value, "inline", [(index, index ^ 1) for index in range(count)])

    def across_to_core(value):
        pairs = [(2 * index + side, 2 * (index ^ 1) + 1 - side) for index in range(count) for side in range(2)]
        return lax.ppermute(value, ("inline", "shot"), pairs)

    def barrier(*values):
        return lax.optimization_barrier(values)

    kept, lent = turn(receiver, half, core)
    y0 = along_y(kept)
    twin = to_core(lent)
    receiver, _ = barrier(receiver, kept)
    there, there_twin = turn(receiver, 1 - half, core)
    moved, moved_twin = across(there), across_to_core(there_twin)
    source, _ = barrier(source, there)
    left, left_lent = turn(source, half, core)
    far, far_lent = turn(source, 1 - half, core)
    left_twin = to_core(left_lent)
    y1 = along_y(twin)
    moved, y0 = barrier(moved, y0)
    y2, z0 = along_y(moved), along_z(y0)
    moved_twin, y1, far, far_lent = barrier(moved_twin, y1, far, far_lent)
    y3, z1 = along_y(moved_twin), along_z(y1)
    right, right_twin = across(far), across_to_core(far_lent)
    z2 = along_z(y2)
    z3 = along_z(y3)
    early = multiply(core, (left, left_twin), (kept, twin, y0, y1, z0, z1))
    middle = multiply(core, (right, right_twin), (moved, moved_twin, y2, y3), (early[0], early[2]))
    middle_came = to_core(middle[1])
    late = multiply(core, (right, right_twin), (z2, z3), (early[1], early[3]))
    late_came = to_core(late[1])
    side = 2 - 4 * odd
    where = jnp.stack([block + shift - core for shift in (0, side, -side) for block in (0, 1)] + [core])
    return spread(scale, cells, where.astype(jnp.int32), (middle[0], middle_came, late[0], late_came))


def on_device(source, receiver):
    shots, cells, times, cross = source.shape
    groups, count = lax.axis_size("shot"), lax.axis_size("inline")
    scale = 1.0 / (times * shots * groups) ** 0.5
    fits = (
        groups == 2
        and count % 4 == 0
        and cross == 2 * LANES
        and shots * times == LANES
        and 4 * cells == LANES
        and times % ROWS == 0
    )
    return routed(source, receiver, scale) if fits else plain(source, receiver, scale)


def solution(mesh):
    placed = (P("shot", "inline", None, None), P("shot", "inline", None, None))
    return jax.shard_map(
        on_device, mesh=mesh, in_specs=placed, out_specs=P(None, "inline", "shot"), check_vma=False
    )
```

```python
import functools

import jax
import jax.numpy as jnp
from jax import lax
from jax.experimental import pallas as pl
from jax.experimental.pallas import tpu as pltpu
from jax.sharding import PartitionSpec as P

LANES = 128
ROWS = 16
VMEM_BYTES = 16 * 1024 * 1024


def shifted(value, axis, steps):
    count = lax.axis_size(axis)
    initial, last = (max(0, -steps), min(count, count - steps))
    return lax.ppermute(value, axis, [(source, source + steps) for source in range(initial, last)])


def band_rows(product, width, lags):
    rows = product.shape[0]
    cross = product.shape[2]
    flat = product.reshape(rows * width, cross)
    flat = jnp.pad(flat, ((0, rows), (0, 0)))
    skewed = flat.reshape(rows, width + 1, cross)[:, :lags, :]
    return jnp.transpose(skewed, (1, 0, 2))


def plain(source, receiver, scale):
    source, receiver = (
        lax.all_to_all(value, "shot", split_axis=3, concat_axis=0, tiled=True) for value in (source, receiver)
    )
    cells = source.shape[1]
    slabs = [receiver if step == 0 else shifted(receiver, "inline", -step) for step in (-2, -1, 0, 1, 2)]
    width = 5 * cells
    product = jnp.einsum(
        "sity,szty->izy", source, jnp.concatenate(slabs, axis=1), preferred_element_type=jnp.float32
    )
    return band_rows(product, width, 4 * cells + 1) * scale


def in_vmem(*values):
    return [pltpu.with_memory_space_constraint(value, pltpu.VMEM) for value in values]


def params():
    return pltpu.CompilerParams(vmem_limit_bytes=VMEM_BYTES)


SCALARS = pl.BlockSpec(memory_space=pltpu.SMEM)
WHOLE = pl.BlockSpec(memory_space=pltpu.VMEM)


def turn_body(which_ref, raw_ref, *refs):
    turned_refs, (buffer_ref, rows_ref, sems) = refs[:4], refs[4:]
    parts, shots, count, times, cross = buffer_ref.shape
    cells = parts * count
    copies = [
        pltpu.make_async_copy(raw_ref.at[:, pl.ds(part * count, count)], buffer_ref.at[part], sems.at[part])
        for part in range(parts)
    ]
    for copy in copies:
        copy.start()
    for part, copy in enumerate(copies):
        copy.wait()
        for cell in range(count):
            for lanes in range(0, cross, LANES):
                tile = buffer_ref[part, :, cell, :, lanes : lanes + LANES].reshape(shots * times, LANES)
                rows_ref[pl.ds(lanes * cells + part * count + cell, LANES, stride=cells), :] = tile.astype(jnp.float32).T
    share = cross // 4 * cells
    half, core = which_ref[0], which_ref[1]
    quarters = [2 * half + core, 2 * half + 1 - core, 2 - 2 * half + core, 3 - 2 * half - core]
    for turned_ref, quarter in zip(turned_refs, quarters):
        rows = rows_ref[pl.ds(pl.multiple_of(quarter * share, share), share), :]
        turned_ref[...] = rows.reshape(turned_ref.shape).astype(turned_ref.dtype)


def turn(raw, which):
    shots, cells, times, cross = raw.shape
    depth = shots * times
    parts = 4
    return pl.pallas_call(
        turn_body,
        in_specs=[SCALARS, pl.BlockSpec(memory_space=pl.ANY)],
        out_specs=[WHOLE] * 4,
        out_shape=[jax.ShapeDtypeStruct((cross // 4, cells, depth), raw.dtype)] * 4,
        scratch_shapes=[
            pltpu.VMEM((parts, shots, cells // parts, times, cross), raw.dtype),
            pltpu.VMEM((cross * cells, depth), jnp.float32),
            pltpu.SemaphoreType.DMA((parts,)),
        ],
        compiler_params=params(),
        cost_estimate=pl.CostEstimate(flops=0, bytes_accessed=raw.size * 4, transcendentals=0),
        name="turn",
    )(which, pltpu.with_memory_space_constraint(raw, pltpu.HBM))


DIMS = (((1,), (1,)), ((), ()))
BLOCK = 8


def multiply_body(pieces, core_ref, *refs):
    slabs = len(pieces)
    sources, right_ref = refs[:2], refs[-1]
    ins = refs[2 : 2 + sum(pieces)]
    share, cells, _ = sources[0].shape
    groups = (slabs * cells + LANES - 1) // LANES
    kept, sent = refs[-1 - 2 * groups : -1 - groups], refs[-1 - groups : -1]
    before = refs[2 + len(ins) : -1 - 2 * groups]
    for place, count in enumerate(pieces):
        side, other = divmod(place, 2)
        slab = 2 * side + (core_ref[0] if other == 0 else 1 - core_ref[0])
        for part in range(count):
            right_ref[slab, part * (share // count) : (part + 1) * (share // count)] = ins[part][...]
        ins = ins[count:]

    @pl.loop(0, share // BLOCK)
    def _(step):
        for place in range(BLOCK):
            cross = step * BLOCK + place
            left = jnp.concatenate([source[cross] for source in sources], axis=0)
            rows = pl.ds(pl.multiple_of(cross * cells, cells), cells)
            for group in range(groups):
                members = range(group * LANES // cells, min(slabs, (group + 1) * LANES // cells))
                right = jnp.concatenate([right_ref[slab, cross] for slab in members], axis=0)
                width = len(members) * cells
                value = lax.dot_general(left, right, DIMS, preferred_element_type=jnp.float32)
                for out, part, first in (
                    (kept[group], value[:cells], group),
                    (sent[group], value[cells:], groups + group),
                ):
                    if before:
                        part = part + before[first][rows, :width]
                    out[rows, :width] = part


def multiply(core, sources, pieces, before=()):
    share, cells, depth = sources[0].shape
    slabs = len(pieces)
    groups = -(-slabs * cells // LANES)
    flops = 2 * share * 2 * cells * slabs * cells * depth
    flat = [part for piece in pieces for part in piece]
    return pl.pallas_call(
        functools.partial(multiply_body, [len(piece) for piece in pieces]),
        in_specs=[SCALARS] + [WHOLE] * (2 + len(flat) + len(before)),
        out_specs=[WHOLE] * (2 * groups),
        out_shape=[jax.ShapeDtypeStruct((share * cells, LANES), jnp.float32)] * (2 * groups),
        scratch_shapes=[pltpu.VMEM((slabs, share, cells, depth), sources[0].dtype)],
        compiler_params=params(),
        cost_estimate=pl.CostEstimate(flops=flops, bytes_accessed=6 << 20, transcendentals=0),
        name="multiply",
    )(core.reshape(1), *in_vmem(*sources, *flat, *before))


def spread_cell(where_ref, cells, cell, kept_ref, came_ref, slabs, factor, skewed_ref):
    kept, came = (ref[pl.ds(cell, LANES // 2, stride=cells), :] for ref in (kept_ref, came_ref))
    core = where_ref[6]
    low = jnp.where(core == 0, kept, came)
    high = jnp.where(core == 0, came, kept)
    turned = jnp.concatenate([low, high], axis=0).T * factor
    for place, slab in enumerate(slabs):
        lag = (where_ref[slab] + 4) * cells - cell
        skewed_ref[pl.ds(lag * cells + cell, cells, stride=cells), :] = turned[cells * place : cells * (place + 1)]


def early_spread_body(scale, cells, where_ref, kept_ref, came_ref, skewed_ref):
    for cell in range(cells):
        spread_cell(where_ref, cells, cell, kept_ref, came_ref, range(4), scale, skewed_ref)


def early_spread(scale, cells, where, products):
    rows = (4 * cells + 1 + 4 * cells) * cells
    return pl.pallas_call(
        functools.partial(early_spread_body, scale, cells),
        in_specs=[SCALARS] + [WHOLE] * 2,
        out_specs=WHOLE,
        out_shape=jax.ShapeDtypeStruct((rows, LANES), jnp.float32),
        compiler_params=params(),
        cost_estimate=pl.CostEstimate(flops=0, bytes_accessed=6 << 20, transcendentals=0),
        name="early_spread",
    )(where, *in_vmem(*products))


def late_spread_body(scale, cells, where_ref, kept_ref, came_ref, _, skewed_ref, image_ref, sems):
    parts = sems.shape[0]
    count = cells // parts
    lags = image_ref.shape[0]
    factor = jnp.where(where_ref[7] == 1, scale, 0.0)
    shaped_ref = skewed_ref.reshape(skewed_ref.shape[0] // cells, cells, LANES)
    copies = []
    for part in range(parts):
        for cell in range(part * count, (part + 1) * count):
            spread_cell(where_ref, cells, cell, kept_ref, came_ref, (4, 5), factor, skewed_ref)
        rows = pl.ds(part * count, count)
        copies.append(
            pltpu.make_async_copy(shaped_ref.at[pl.ds(2 * cells, lags), rows], image_ref.at[:, rows], sems.at[part])
        )
        copies[-1].start()
    for copy in copies:
        copy.wait()


def late_spread(scale, cells, where, products, skewed):
    lags = 4 * cells + 1
    return pl.pallas_call(
        functools.partial(late_spread_body, scale, cells),
        in_specs=[SCALARS] + [WHOLE] * 3,
        out_specs=[WHOLE, pl.BlockSpec(memory_space=pl.ANY)],
        out_shape=[
            jax.ShapeDtypeStruct(skewed.shape, jnp.float32),
            jax.ShapeDtypeStruct((lags, cells, LANES), jnp.float32),
        ],
        input_output_aliases={3: 0},
        scratch_shapes=[pltpu.SemaphoreType.DMA((4,))],
        compiler_params=params(),
        name="late_spread",
    )(where, *in_vmem(*products, skewed))[1]


def routed(source, receiver, scale):
    count = lax.axis_size("inline")
    cells = source.shape[1]
    own = lax.axis_index("inline")
    core, odd = own & 1, (own >> 1) & 1
    half = lax.axis_index("shot")

    def across(value):
        return lax.ppermute(value, "shot", [(0, 1), (1, 0)])

    def along_y(value):
        return lax.ppermute(value, "inline", [(index, index ^ 2) for index in range(count)])

    def along_z(value):
        steps = (4, -4)
        return lax.ppermute(
            value, "inline", [(index, (index + steps[index // 2 % 2]) % count) for index in range(count)]
        )

    def to_core(value):
        return lax.ppermute(value, "inline", [(index, index ^ 1) for index in range(count)])

    def across_to_core(value):
        pairs = [(2 * index + side, 2 * (index ^ 1) + 1 - side) for index in range(count) for side in range(2)]
        return lax.ppermute(value, ("inline", "shot"), pairs)

    def barrier(*values):
        return lax.optimization_barrier(values)

    which = jnp.stack([half, core]).astype(jnp.int32)
    kept, lent, there, there_twin = turn(receiver, which)
    y0 = along_y(kept)
    twin = to_core(lent)
    moved, moved_twin = across(there), across_to_core(there_twin)
    source, _ = barrier(source, kept)
    left, left_lent, far, far_lent = turn(source, which)
    left_twin = to_core(left_lent)
    y1 = along_y(twin)
    moved, y0 = barrier(moved, y0)
    y2, z0 = along_y(moved), along_z(y0)
    moved_twin, y1, far, far_lent = barrier(moved_twin, y1, far, far_lent)
    middle_share = moved_twin.shape[0] // 2
    y3 = [along_y(moved_twin[:middle_share]), along_y(moved_twin[middle_share:])]
    z1 = along_z(y1)
    right, right_twin = across(far), across_to_core(far_lent)
    z2 = along_z(y2)
    early = multiply(core, (left, left_twin), [(piece,) for piece in (kept, twin, y0, y1, z0, z1)])
    y3[1], *early = barrier(y3[1], *early)
    z3 = [along_z(part) for part in y3]
    middle = multiply(core, (right, right_twin), ((moved,), (moved_twin,), (y2,), y3), (early[0], early[2]))
    middle_came = to_core(middle[1])
    side = 2 - 4 * odd
    end = jnp.where(odd == 0, own >> 1 == 0, own >> 1 == count // 2 - 1)
    where = jnp.stack([block + shift - core for shift in (0, side, -side) for block in (0, 1)] + [core, 1 - end])
    where = where.astype(jnp.int32)
    skewed = early_spread(scale, cells, where, (middle[0], middle_came))
    late = multiply(core, (right, right_twin), ((z2,), z3), (early[1], early[3]))
    late_came = to_core(late[1])
    return late_spread(scale, cells, where, (late[0], late_came), skewed)


def on_device(source, receiver):
    shots, cells, times, cross = source.shape
    groups, count = lax.axis_size("shot"), lax.axis_size("inline")
    scale = 1.0 / (times * shots * groups) ** 0.5
    fits = (
        groups == 2
        and count % 4 == 0
        and cross == 2 * LANES
        and shots * times == LANES
        and 4 * cells == LANES
        and times % ROWS == 0
    )
    return routed(source, receiver, scale) if fits else plain(source, receiver, scale)


def solution(mesh):
    placed = (P("shot", "inline", None, None), P("shot", "inline", None, None))
    return jax.shard_map(
        on_device, mesh=mesh, in_specs=placed, out_specs=P(None, "inline", "shot"), check_vma=False
    )
```

```python
import functools

import jax
import jax.numpy as jnp
from jax import lax
from jax.experimental import pallas as pl
from jax.experimental.pallas import tpu as pltpu
from jax.sharding import PartitionSpec as P

LANES = 128
ROWS = 16
VMEM_BYTES = 24 * 1024 * 1024


def shifted(value, axis, steps):
    count = lax.axis_size(axis)
    initial, last = (max(0, -steps), min(count, count - steps))
    return lax.ppermute(value, axis, [(source, source + steps) for source in range(initial, last)])


def band_rows(product, width, lags):
    rows = product.shape[0]
    cross = product.shape[2]
    flat = product.reshape(rows * width, cross)
    flat = jnp.pad(flat, ((0, rows), (0, 0)))
    skewed = flat.reshape(rows, width + 1, cross)[:, :lags, :]
    return jnp.transpose(skewed, (1, 0, 2))


def plain(source, receiver, scale):
    source, receiver = (
        lax.all_to_all(value, "shot", split_axis=3, concat_axis=0, tiled=True) for value in (source, receiver)
    )
    cells = source.shape[1]
    slabs = [receiver if step == 0 else shifted(receiver, "inline", -step) for step in (-2, -1, 0, 1, 2)]
    width = 5 * cells
    product = jnp.einsum(
        "sity,szty->izy", source, jnp.concatenate(slabs, axis=1), preferred_element_type=jnp.float32
    )
    return band_rows(product, width, 4 * cells + 1) * scale


GAP = 3


def apart(count):
    stride = GAP * count
    return stride + 1 - stride % 2


def in_vmem(*values):
    return [pltpu.with_memory_space_constraint(value, pltpu.VMEM) for value in values]


def params():
    return pltpu.CompilerParams(vmem_limit_bytes=VMEM_BYTES)


SCALARS = pl.BlockSpec(memory_space=pltpu.SMEM)
WHOLE = pl.BlockSpec(memory_space=pltpu.VMEM)


def turn_body(which_ref, raw_ref, *refs):
    turned_refs, (buffer_ref, rows_ref, sems) = refs[:4], refs[4:]
    parts, shots, count, times, cross = buffer_ref.shape
    cells = parts * count
    copies = [
        pltpu.make_async_copy(raw_ref.at[:, pl.ds(part * count, count)], buffer_ref.at[part], sems.at[part])
        for part in range(parts)
    ]
    for copy in copies:
        copy.start()
    for part, copy in enumerate(copies):
        copy.wait()
        for cell in range(count):
            for lanes in range(0, cross, LANES):
                tile = buffer_ref[part, :, cell, :, lanes : lanes + LANES].reshape(shots * times, LANES)
                base = lanes * apart(cells) + GAP * (part * count + cell)
                rows_ref[pl.ds(base, LANES, stride=apart(cells)), :] = tile.astype(jnp.float32).T
    half, core = which_ref[0], which_ref[1]
    quarters = [2 * half + core, 2 * half + 1 - core, 2 - 2 * half + core, 3 - 2 * half - core]
    for turned_ref, quarter in zip(turned_refs, quarters):
        share = turned_ref.shape[0]
        for place in range(share):
            base = (quarter * share + place) * apart(cells)
            turned_ref[place] = rows_ref[pl.ds(base, cells, stride=GAP), :].astype(turned_ref.dtype)


def turn(raw, which):
    shots, cells, times, cross = raw.shape
    depth = shots * times
    parts = 4
    return pl.pallas_call(
        turn_body,
        in_specs=[SCALARS, pl.BlockSpec(memory_space=pl.ANY)],
        out_specs=[WHOLE] * 4,
        out_shape=[jax.ShapeDtypeStruct((cross // 4, cells, depth), raw.dtype)] * 4,
        scratch_shapes=[
            pltpu.VMEM((parts, shots, cells // parts, times, cross), raw.dtype),
            pltpu.VMEM((cross * apart(cells), depth), jnp.float32),
            pltpu.SemaphoreType.DMA((parts,)),
        ],
        compiler_params=params(),
        cost_estimate=pl.CostEstimate(flops=0, bytes_accessed=raw.size * 4, transcendentals=0),
        name="turn",
    )(which, pltpu.with_memory_space_constraint(raw, pltpu.HBM))


DIMS = (((1,), (1,)), ((), ()))
BLOCK = 8


def multiply_body(pieces, core_ref, *refs):
    slabs = len(pieces)
    sources, right_ref = refs[:2], refs[-1]
    ins = refs[2 : 2 + sum(pieces)]
    share, cells, _ = sources[0].shape
    groups = (slabs * cells + LANES - 1) // LANES
    kept, sent = refs[-1 - 2 * groups : -1 - groups], refs[-1 - groups : -1]
    before = refs[2 + len(ins) : -1 - 2 * groups]
    for place, count in enumerate(pieces):
        side, other = divmod(place, 2)
        slab = 2 * side + (core_ref[0] if other == 0 else 1 - core_ref[0])
        for part in range(count):
            right_ref[slab, part * (share // count) : (part + 1) * (share // count)] = ins[part][...]
        ins = ins[count:]

    @pl.loop(0, share // BLOCK)
    def _(step):
        for place in range(BLOCK):
            cross = step * BLOCK + place
            left = jnp.concatenate([source[cross] for source in sources], axis=0)
            rows = pl.ds(pl.multiple_of(cross * cells, cells), cells)
            for group in range(groups):
                members = range(group * LANES // cells, min(slabs, (group + 1) * LANES // cells))
                right = jnp.concatenate([right_ref[slab, cross] for slab in members], axis=0)
                width = len(members) * cells
                value = lax.dot_general(left, right, DIMS, preferred_element_type=jnp.float32)
                for out, part, first in (
                    (kept[group], value[:cells], group),
                    (sent[group], value[cells:], groups + group),
                ):
                    if before:
                        part = part + before[first][rows, :width]
                    out[rows, :width] = part


def multiply(core, sources, pieces, before=()):
    share, cells, depth = sources[0].shape
    slabs = len(pieces)
    groups = -(-slabs * cells // LANES)
    flops = 2 * share * 2 * cells * slabs * cells * depth
    flat = [part for piece in pieces for part in piece]
    return pl.pallas_call(
        functools.partial(multiply_body, [len(piece) for piece in pieces]),
        in_specs=[SCALARS] + [WHOLE] * (2 + len(flat) + len(before)),
        out_specs=[WHOLE] * (2 * groups),
        out_shape=[jax.ShapeDtypeStruct((share * cells, LANES), jnp.float32)] * (2 * groups),
        scratch_shapes=[pltpu.VMEM((slabs, share, cells, depth), sources[0].dtype)],
        compiler_params=params(),
        cost_estimate=pl.CostEstimate(flops=flops, bytes_accessed=6 << 20, transcendentals=0),
        name="multiply",
    )(core.reshape(1), *in_vmem(*sources, *flat, *before))


def gather_rows(where_ref, cells, kept_ref, came_ref, rows_ref):
    share = kept_ref.shape[0] // cells
    for ref, first in ((kept_ref, where_ref[6] * share), (came_ref, (1 - where_ref[6]) * share)):
        for place in range(share):
            base = (first + place) * apart(cells)
            rows_ref[pl.ds(base, cells, stride=GAP), :] = ref[place * cells : (place + 1) * cells, :]


def spread_rows(where_ref, cells, slabs, factor, rows_ref, skewed_ref):
    line = skewed_ref.shape[0] // cells
    for cell in range(cells):
        turned = rows_ref[pl.ds(GAP * cell, LANES, stride=apart(cells)), :].T * factor
        for place, slab in enumerate(slabs):
            base = cell * line + GAP * ((where_ref[slab] + 4) * cells - cell)
            skewed_ref[pl.ds(base, cells, stride=GAP), :] = turned[cells * place : cells * (place + 1)]


def early_spread_body(scale, cells, where_ref, kept_ref, came_ref, skewed_ref, rows_ref):
    gather_rows(where_ref, cells, kept_ref, came_ref, rows_ref)
    spread_rows(where_ref, cells, range(4), scale, rows_ref, skewed_ref)


def early_spread(scale, cells, where, products):
    rows = apart(4 * cells + 1 + 4 * cells) * cells
    return pl.pallas_call(
        functools.partial(early_spread_body, scale, cells),
        in_specs=[SCALARS] + [WHOLE] * 2,
        out_specs=WHOLE,
        out_shape=jax.ShapeDtypeStruct((rows, LANES), jnp.float32),
        scratch_shapes=[pltpu.VMEM((LANES * apart(cells), LANES), jnp.float32)],
        compiler_params=params(),
        cost_estimate=pl.CostEstimate(flops=0, bytes_accessed=6 << 20, transcendentals=0),
        name="early_spread",
    )(where, *in_vmem(*products))


def late_spread_body(scale, cells, where_ref, kept_ref, came_ref, _, skewed_ref, image_ref, rows_ref, buffer_ref, sems):
    factor = jnp.where(where_ref[7] == 1, scale, 0.0)
    gather_rows(where_ref, cells, kept_ref, came_ref, rows_ref)
    spread_rows(where_ref, cells, (4, 5), factor, rows_ref, skewed_ref)
    line = skewed_ref.shape[0] // cells
    parts, lags = sems.shape[0], image_ref.shape[0]
    cuts = [lags * part // parts for part in range(parts + 1)]
    copies = []
    for part, (start, stop) in enumerate(zip(cuts, cuts[1:])):
        for lag in range(start, stop):
            buffer_ref[lag] = skewed_ref[pl.ds(GAP * (2 * cells + lag), cells, stride=line), :]
        block = pl.ds(start, stop - start)
        copies.append(pltpu.make_async_copy(buffer_ref.at[block], image_ref.at[block], sems.at[part]))
        copies[-1].start()
    for copy in copies:
        copy.wait()


def late_spread(scale, cells, where, products, skewed):
    lags = 4 * cells + 1
    return pl.pallas_call(
        functools.partial(late_spread_body, scale, cells),
        in_specs=[SCALARS] + [WHOLE] * 3,
        out_specs=[WHOLE, pl.BlockSpec(memory_space=pl.ANY)],
        out_shape=[
            jax.ShapeDtypeStruct(skewed.shape, jnp.float32),
            jax.ShapeDtypeStruct((lags, cells, LANES), jnp.float32),
        ],
        input_output_aliases={3: 0},
        scratch_shapes=[
            pltpu.VMEM((LANES * apart(cells), LANES), jnp.float32),
            pltpu.VMEM((lags, cells, LANES), jnp.float32),
            pltpu.SemaphoreType.DMA((4,)),
        ],
        compiler_params=params(),
        name="late_spread",
    )(where, *in_vmem(*products, skewed))[1]


def routed(source, receiver, scale):
    count = lax.axis_size("inline")
    cells = source.shape[1]
    own = lax.axis_index("inline")
    core, odd = own & 1, (own >> 1) & 1
    half = lax.axis_index("shot")

    def across(value):
        return lax.ppermute(value, "shot", [(0, 1), (1, 0)])

    def along_y(value):
        return lax.ppermute(value, "inline", [(index, index ^ 2) for index in range(count)])

    def along_z(value):
        steps = (4, -4)
        return lax.ppermute(
            value, "inline", [(index, (index + steps[index // 2 % 2]) % count) for index in range(count)]
        )

    def to_core(value):
        return lax.ppermute(value, "inline", [(index, index ^ 1) for index in range(count)])

    def across_to_core(value):
        pairs = [(2 * index + side, 2 * (index ^ 1) + 1 - side) for index in range(count) for side in range(2)]
        return lax.ppermute(value, ("inline", "shot"), pairs)

    def barrier(*values):
        return lax.optimization_barrier(values)

    which = jnp.stack([half, core]).astype(jnp.int32)
    kept, lent, there, there_twin = turn(receiver, which)
    y0 = along_y(kept)
    twin = to_core(lent)
    there, twin = barrier(there, twin)
    moved = across(there)
    y1 = along_y(twin)
    source, _ = barrier(source, twin)
    left, left_lent, far, far_lent = turn(source, which)
    moved, y0, there_twin, left_lent = barrier(moved, y0, there_twin, left_lent)
    left_twin = to_core(left_lent)
    y2, z0 = along_y(moved), along_z(y0)
    moved_twin = across_to_core(there_twin)
    moved_twin, y1, far, far_lent = barrier(moved_twin, y1, far, far_lent)
    y3, z1 = along_y(moved_twin), along_z(y1)
    right, right_twin = across(far), across_to_core(far_lent)
    z2 = along_z(y2)
    early = multiply(core, (left, left_twin), [(piece,) for piece in (kept, twin, y0, y1, z0, z1)])
    y3, *early = barrier(y3, *early)
    z3 = along_z(y3)
    middle = multiply(core, (right, right_twin), ((moved,), (moved_twin,), (y2,), (y3,)), (early[0], early[2]))
    middle_came = to_core(middle[1])
    side = 2 - 4 * odd
    end = jnp.where(odd == 0, own >> 1 == 0, own >> 1 == count // 2 - 1)
    where = jnp.stack([block + shift - core for shift in (0, side, -side) for block in (0, 1)] + [core, 1 - end])
    where = where.astype(jnp.int32)
    skewed = early_spread(scale, cells, where, (middle[0], middle_came))
    late = multiply(core, (right, right_twin), ((z2,), (z3,)), (early[1], early[3]))
    late_came = to_core(late[1])
    return late_spread(scale, cells, where, (late[0], late_came), skewed)


def on_device(source, receiver):
    shots, cells, times, cross = source.shape
    groups, count = lax.axis_size("shot"), lax.axis_size("inline")
    scale = 1.0 / (times * shots * groups) ** 0.5
    fits = (
        groups == 2
        and count % 4 == 0
        and cross == 2 * LANES
        and shots * times == LANES
        and 4 * cells == LANES
        and times % ROWS == 0
    )
    return routed(source, receiver, scale) if fits else plain(source, receiver, scale)


def solution(mesh):
    placed = (P("shot", "inline", None, None), P("shot", "inline", None, None))
    return jax.shard_map(
        on_device, mesh=mesh, in_specs=placed, out_specs=P(None, "inline", "shot"), check_vma=False
    )
```

```python
import functools

import jax
import jax.numpy as jnp
from jax import lax
from jax.experimental import pallas as pl
from jax.experimental.pallas import tpu as pltpu
from jax.sharding import PartitionSpec as P

LANES = 128
ROWS = 16
VMEM_BYTES = 24 * 1024 * 1024


def shifted(value, axis, steps):
    count = lax.axis_size(axis)
    initial, last = (max(0, -steps), min(count, count - steps))
    return lax.ppermute(value, axis, [(source, source + steps) for source in range(initial, last)])


def band_rows(product, width, lags):
    rows = product.shape[0]
    cross = product.shape[2]
    flat = product.reshape(rows * width, cross)
    flat = jnp.pad(flat, ((0, rows), (0, 0)))
    skewed = flat.reshape(rows, width + 1, cross)[:, :lags, :]
    return jnp.transpose(skewed, (1, 0, 2))


def plain(source, receiver, scale):
    source, receiver = (
        lax.all_to_all(value, "shot", split_axis=3, concat_axis=0, tiled=True) for value in (source, receiver)
    )
    cells = source.shape[1]
    slabs = [receiver if step == 0 else shifted(receiver, "inline", -step) for step in (-2, -1, 0, 1, 2)]
    width = 5 * cells
    product = jnp.einsum(
        "sity,szty->izy", source, jnp.concatenate(slabs, axis=1), preferred_element_type=jnp.float32
    )
    return band_rows(product, width, 4 * cells + 1) * scale


GAP = 3


def apart(count):
    stride = GAP * count
    return stride + 1 - stride % 2


def in_vmem(*values):
    return [pltpu.with_memory_space_constraint(value, pltpu.VMEM) for value in values]


def params():
    return pltpu.CompilerParams(vmem_limit_bytes=VMEM_BYTES)


SCALARS = pl.BlockSpec(memory_space=pltpu.SMEM)
WHOLE = pl.BlockSpec(memory_space=pltpu.VMEM)


def turn_body(which_ref, raw_ref, *refs):
    turned_refs, (buffer_ref, rows_ref, sems) = refs[:4], refs[4:]
    parts, shots, count, times, cross = buffer_ref.shape
    cells = parts * count
    copies = [
        pltpu.make_async_copy(raw_ref.at[:, pl.ds(part * count, count)], buffer_ref.at[part], sems.at[part])
        for part in range(parts)
    ]
    for copy in copies:
        copy.start()
    for part, copy in enumerate(copies):
        copy.wait()
        for cell in range(count):
            for lanes in range(0, cross, LANES):
                tile = buffer_ref[part, :, cell, :, lanes : lanes + LANES].reshape(shots * times, LANES)
                base = lanes * apart(cells) + GAP * (part * count + cell)
                rows_ref[pl.ds(base, LANES, stride=apart(cells)), :] = tile.astype(jnp.float32).T
    half, core = which_ref[0], which_ref[1]
    quarters = [2 * half + core, 2 * half + 1 - core, 2 - 2 * half + core, 3 - 2 * half - core]
    for turned_ref, quarter in zip(turned_refs, quarters):
        share = turned_ref.shape[0]
        for place in range(share):
            base = (quarter * share + place) * apart(cells)
            turned_ref[place] = rows_ref[pl.ds(base, cells, stride=GAP), :].astype(turned_ref.dtype)


def turn(raw, which):
    shots, cells, times, cross = raw.shape
    depth = shots * times
    parts = 4
    return pl.pallas_call(
        turn_body,
        in_specs=[SCALARS, pl.BlockSpec(memory_space=pl.ANY)],
        out_specs=[WHOLE] * 4,
        out_shape=[jax.ShapeDtypeStruct((cross // 4, cells, depth), raw.dtype)] * 4,
        scratch_shapes=[
            pltpu.VMEM((parts, shots, cells // parts, times, cross), raw.dtype),
            pltpu.VMEM((cross * apart(cells), depth), jnp.float32),
            pltpu.SemaphoreType.DMA((parts,)),
        ],
        compiler_params=params(),
        cost_estimate=pl.CostEstimate(flops=0, bytes_accessed=raw.size * 4, transcendentals=0),
        name="turn",
    )(which, pltpu.with_memory_space_constraint(raw, pltpu.HBM))


DIMS = (((1,), (1,)), ((), ()))
BLOCK = 8


def multiply_body(pieces, core_ref, *refs):
    slabs = len(pieces)
    sources, right_ref = refs[:2], refs[-1]
    ins = refs[2 : 2 + sum(pieces)]
    share, cells, _ = sources[0].shape
    groups = (slabs * cells + LANES - 1) // LANES
    kept, sent = refs[-1 - 2 * groups : -1 - groups], refs[-1 - groups : -1]
    before = refs[2 + len(ins) : -1 - 2 * groups]
    for place, count in enumerate(pieces):
        side, other = divmod(place, 2)
        slab = 2 * side + (core_ref[0] if other == 0 else 1 - core_ref[0])
        for part in range(count):
            right_ref[slab, part * (share // count) : (part + 1) * (share // count)] = ins[part][...]
        ins = ins[count:]

    @pl.loop(0, share // BLOCK)
    def _(step):
        for place in range(BLOCK):
            cross = step * BLOCK + place
            left = jnp.concatenate([source[cross] for source in sources], axis=0)
            rows = pl.ds(pl.multiple_of(cross * cells, cells), cells)
            for group in range(groups):
                members = range(group * LANES // cells, min(slabs, (group + 1) * LANES // cells))
                right = jnp.concatenate([right_ref[slab, cross] for slab in members], axis=0)
                width = len(members) * cells
                value = lax.dot_general(left, right, DIMS, preferred_element_type=jnp.float32)
                for out, part, first in (
                    (kept[group], value[:cells], group),
                    (sent[group], value[cells:], groups + group),
                ):
                    if before:
                        part = part + before[first][rows, :width]
                    out[rows, :width] = part


def multiply(core, sources, pieces, before=()):
    share, cells, depth = sources[0].shape
    slabs = len(pieces)
    groups = -(-slabs * cells // LANES)
    flops = 2 * share * 2 * cells * slabs * cells * depth
    flat = [part for piece in pieces for part in piece]
    return pl.pallas_call(
        functools.partial(multiply_body, [len(piece) for piece in pieces]),
        in_specs=[SCALARS] + [WHOLE] * (2 + len(flat) + len(before)),
        out_specs=[WHOLE] * (2 * groups),
        out_shape=[jax.ShapeDtypeStruct((share * cells, LANES), jnp.float32)] * (2 * groups),
        scratch_shapes=[pltpu.VMEM((slabs, share, cells, depth), sources[0].dtype)],
        compiler_params=params(),
        cost_estimate=pl.CostEstimate(flops=flops, bytes_accessed=6 << 20, transcendentals=0),
        name="multiply",
    )(core.reshape(1), *in_vmem(*sources, *flat, *before))


def gather_rows(where_ref, cells, kept_ref, came_ref, rows_ref):
    share = kept_ref.shape[0] // cells
    for ref, first in ((kept_ref, where_ref[6] * share), (came_ref, (1 - where_ref[6]) * share)):
        for place in range(share):
            base = (first + place) * apart(cells)
            rows_ref[pl.ds(base, cells, stride=GAP), :] = ref[place * cells : (place + 1) * cells, :]


def spread_rows(where_ref, cells, slabs, factor, rows_ref, skewed_ref):
    line = skewed_ref.shape[0] // cells
    for cell in range(cells):
        turned = rows_ref[pl.ds(GAP * cell, LANES, stride=apart(cells)), :].T * factor
        for place, slab in enumerate(slabs):
            base = cell * line + GAP * ((where_ref[slab] + 4) * cells - cell)
            skewed_ref[pl.ds(base, cells, stride=GAP), :] = turned[cells * place : cells * (place + 1)]


def early_spread_body(scale, cells, where_ref, kept_ref, came_ref, skewed_ref, rows_ref):
    gather_rows(where_ref, cells, kept_ref, came_ref, rows_ref)
    spread_rows(where_ref, cells, range(4), scale, rows_ref, skewed_ref)


def early_spread(scale, cells, where, products):
    rows = apart(4 * cells + 1 + 4 * cells) * cells
    return pl.pallas_call(
        functools.partial(early_spread_body, scale, cells),
        in_specs=[SCALARS] + [WHOLE] * 2,
        out_specs=WHOLE,
        out_shape=jax.ShapeDtypeStruct((rows, LANES), jnp.float32),
        scratch_shapes=[pltpu.VMEM((LANES * apart(cells), LANES), jnp.float32)],
        compiler_params=params(),
        cost_estimate=pl.CostEstimate(flops=0, bytes_accessed=6 << 20, transcendentals=0),
        name="early_spread",
    )(where, *in_vmem(*products))


def late_spread_body(scale, cells, where_ref, kept_ref, came_ref, _, skewed_ref, image_ref, rows_ref, buffer_ref, sems):
    gather_rows(where_ref, cells, kept_ref, came_ref, rows_ref)
    spread_rows(where_ref, cells, (4, 5), scale, rows_ref, skewed_ref)
    line = skewed_ref.shape[0] // cells
    parts, lags = sems.shape[0], image_ref.shape[0]
    cuts = [lags * part // parts for part in range(parts + 1)]
    copies = []
    for part, (start, stop) in enumerate(zip(cuts, cuts[1:])):
        for lag in range(start, stop):
            buffer_ref[lag] = skewed_ref[pl.ds(GAP * (2 * cells + lag), cells, stride=line), :]
        block = pl.ds(start, stop - start)
        copies.append(pltpu.make_async_copy(buffer_ref.at[block], image_ref.at[block], sems.at[part]))
        copies[-1].start()
    for copy in copies:
        copy.wait()


def late_spread(scale, cells, where, products, skewed):
    lags = 4 * cells + 1
    return pl.pallas_call(
        functools.partial(late_spread_body, scale, cells),
        in_specs=[SCALARS] + [WHOLE] * 3,
        out_specs=[WHOLE, pl.BlockSpec(memory_space=pl.ANY)],
        out_shape=[
            jax.ShapeDtypeStruct(skewed.shape, jnp.float32),
            jax.ShapeDtypeStruct((lags, cells, LANES), jnp.float32),
        ],
        input_output_aliases={3: 0},
        scratch_shapes=[
            pltpu.VMEM((LANES * apart(cells), LANES), jnp.float32),
            pltpu.VMEM((lags, cells, LANES), jnp.float32),
            pltpu.SemaphoreType.DMA((4,)),
        ],
        compiler_params=params(),
        name="late_spread",
    )(where, *in_vmem(*products, skewed))[1]


def routed(source, receiver, scale):
    count = lax.axis_size("inline")
    cells = source.shape[1]
    own = lax.axis_index("inline")
    core, odd = own & 1, (own >> 1) & 1
    half = lax.axis_index("shot")

    def across(value):
        return lax.ppermute(value, "shot", [(0, 1), (1, 0)])

    def along_y(value):
        return lax.ppermute(value, "inline", [(index, index ^ 2) for index in range(count)])

    def along_z(value):
        pairs = [(index, index + (4, -4)[index // 2 % 2]) for index in range(count)]
        return lax.ppermute(value, "inline", [pair for pair in pairs if 0 <= pair[1] < count])

    def to_core(value):
        return lax.ppermute(value, "inline", [(index, index ^ 1) for index in range(count)])

    def across_to_core(value):
        pairs = [(2 * index + side, 2 * (index ^ 1) + 1 - side) for index in range(count) for side in range(2)]
        return lax.ppermute(value, ("inline", "shot"), pairs)

    def barrier(*values):
        return lax.optimization_barrier(values)

    which = jnp.stack([half, core]).astype(jnp.int32)
    kept, lent, there, there_twin = turn(receiver, which)
    y0 = along_y(kept)
    twin = to_core(lent)
    there, there_twin, twin = barrier(there, there_twin, twin)
    moved, moved_twin = across(there), across_to_core(there_twin)
    y1 = along_y(twin)
    source, _ = barrier(source, twin)
    left, left_lent, far, far_lent = turn(source, which)
    moved, y0, left = barrier(moved, y0, left)
    y2, z0 = along_y(moved), along_z(y0)
    moved_twin, y1, far, left_lent = barrier(moved_twin, y1, far, left_lent)
    y3, z1 = along_y(moved_twin), along_z(y1)
    left_twin = to_core(left_lent)
    right = across(far)
    z0, far_lent, y2 = barrier(z0, far_lent, y2)
    right_twin = across_to_core(far_lent)
    z2 = along_z(y2)
    left_twin, right = barrier(left_twin, right)
    early = multiply(core, (left, left_twin), [(piece,) for piece in (kept, twin, y0, y1, z0, z1)])
    y3, *early = barrier(y3, *early)
    z3 = along_z(y3)
    middle = multiply(core, (right, right_twin), ((moved,), (moved_twin,), (y2,), (y3,)), (early[0], early[2]))
    middle_came = to_core(middle[1])
    side = 2 - 4 * odd
    where = jnp.stack([block + shift - core for shift in (0, side, -side) for block in (0, 1)] + [core])
    where = where.astype(jnp.int32)
    skewed = early_spread(scale, cells, where, (middle[0], middle_came))
    late = multiply(core, (right, right_twin), ((z2,), (z3,)), (early[1], early[3]))
    late_came = to_core(late[1])
    return late_spread(scale, cells, where, (late[0], late_came), skewed)


def on_device(source, receiver):
    shots, cells, times, cross = source.shape
    groups, count = lax.axis_size("shot"), lax.axis_size("inline")
    scale = 1.0 / (times * shots * groups) ** 0.5
    fits = (
        groups == 2
        and count % 4 == 0
        and cross == 2 * LANES
        and shots * times == LANES
        and 4 * cells == LANES
        and times % ROWS == 0
    )
    return routed(source, receiver, scale) if fits else plain(source, receiver, scale)


def solution(mesh):
    placed = (P("shot", "inline", None, None), P("shot", "inline", None, None))
    return jax.shard_map(
        on_device, mesh=mesh, in_specs=placed, out_specs=P(None, "inline", "shot"), check_vma=False
    )
```

```python
import functools

import jax
import jax.numpy as jnp
from jax import lax
from jax.experimental import pallas as pl
from jax.experimental.pallas import tpu as pltpu
from jax.sharding import PartitionSpec as P

LANES = 128
ROWS = 16
VMEM_BYTES = 24 * 1024 * 1024


def shifted(value, axis, steps):
    count = lax.axis_size(axis)
    initial, last = (max(0, -steps), min(count, count - steps))
    return lax.ppermute(value, axis, [(source, source + steps) for source in range(initial, last)])


def band_rows(product, width, lags):
    rows = product.shape[0]
    cross = product.shape[2]
    flat = product.reshape(rows * width, cross)
    flat = jnp.pad(flat, ((0, rows), (0, 0)))
    skewed = flat.reshape(rows, width + 1, cross)[:, :lags, :]
    return jnp.transpose(skewed, (1, 0, 2))


def plain(source, receiver, scale):
    source, receiver = (
        lax.all_to_all(value, "shot", split_axis=3, concat_axis=0, tiled=True) for value in (source, receiver)
    )
    cells = source.shape[1]
    slabs = [receiver if step == 0 else shifted(receiver, "inline", -step) for step in (-2, -1, 0, 1, 2)]
    width = 5 * cells
    product = jnp.einsum(
        "sity,szty->izy", source, jnp.concatenate(slabs, axis=1), preferred_element_type=jnp.float32
    )
    return band_rows(product, width, 4 * cells + 1) * scale


GAP = 3


def apart(count):
    stride = GAP * count
    return stride + 1 - stride % 2


def in_vmem(*values):
    return [pltpu.with_memory_space_constraint(value, pltpu.VMEM) for value in values]


def params():
    return pltpu.CompilerParams(vmem_limit_bytes=VMEM_BYTES)


SCALARS = pl.BlockSpec(memory_space=pltpu.SMEM)
WHOLE = pl.BlockSpec(memory_space=pltpu.VMEM)


def turn_body(which_ref, raw_ref, *refs):
    turned_refs, (buffer_ref, rows_ref, sems) = refs[:4], refs[4:]
    parts, shots, count, times, cross = buffer_ref.shape
    cells = parts * count
    copies = [
        pltpu.make_async_copy(raw_ref.at[:, pl.ds(part * count, count)], buffer_ref.at[part], sems.at[part])
        for part in range(parts)
    ]
    for copy in copies:
        copy.start()
    for part, copy in enumerate(copies):
        copy.wait()
        for cell in range(count):
            for lanes in range(0, cross, LANES):
                tile = buffer_ref[part, :, cell, :, lanes : lanes + LANES].reshape(shots * times, LANES)
                base = lanes * apart(cells) + GAP * (part * count + cell)
                rows_ref[pl.ds(base, LANES, stride=apart(cells)), :] = tile.astype(jnp.float32).T
    half, core = which_ref[0], which_ref[1]
    quarters = [2 * half + core, 2 * half + 1 - core, 2 - 2 * half + core, 3 - 2 * half - core]
    for turned_ref, quarter in zip(turned_refs, quarters):
        share = turned_ref.shape[0]
        for place in range(share):
            base = (quarter * share + place) * apart(cells)
            turned_ref[place] = rows_ref[pl.ds(base, cells, stride=GAP), :].astype(turned_ref.dtype)


def turn(raw, which):
    shots, cells, times, cross = raw.shape
    depth = shots * times
    chunks = 4
    return pl.pallas_call(
        turn_body,
        in_specs=[SCALARS, pl.BlockSpec(memory_space=pl.ANY)],
        out_specs=[WHOLE] * 4,
        out_shape=[jax.ShapeDtypeStruct((cross // 4, cells, depth), raw.dtype)] * 4,
        scratch_shapes=[
            pltpu.VMEM((chunks, shots, cells // chunks, times, cross), raw.dtype),
            pltpu.VMEM((cross * apart(cells), depth), jnp.float32),
            pltpu.SemaphoreType.DMA((chunks,)),
        ],
        compiler_params=params(),
        cost_estimate=pl.CostEstimate(flops=0, bytes_accessed=raw.size * 4, transcendentals=0),
        name="turn",
    )(which, pltpu.with_memory_space_constraint(raw, pltpu.HBM))


DIMS = (((1,), (1,)), ((), ()))


def multiply_body(pieces, core_ref, *refs):
    own, *pieces = pieces
    slabs = len(pieces)
    sources, right_ref = (refs[:own], refs[own]), refs[-1]
    ins = refs[own + 1 : own + 1 + sum(pieces)]
    share, cells, _ = refs[own].shape
    groups = (slabs * cells + LANES - 1) // LANES
    kept, sent = refs[-1 - 2 * groups : -1 - groups], refs[-1 - groups : -1]
    before = refs[own + 1 + len(ins) : -1 - 2 * groups]
    for place, count in enumerate(pieces):
        side, other = divmod(place, 2)
        slab = 2 * side + (core_ref[0] if other == 0 else 1 - core_ref[0])
        for part in range(count):
            right_ref[slab, part * (share // count) : (part + 1) * (share // count)] = ins[part][...]
        ins = ins[count:]

    for cross_part in range(own):
        first_cross = cross_part * (share // own)
        for place in range(share // own):
            cross = first_cross + place
            left = jnp.concatenate([sources[0][cross_part][place], sources[1][cross]], axis=0)
            rows = pl.ds(cross * cells, cells)
            for group in range(groups):
                members = range(group * LANES // cells, min(slabs, (group + 1) * LANES // cells))
                right = jnp.concatenate([right_ref[slab, cross] for slab in members], axis=0)
                width = len(members) * cells
                value = lax.dot_general(left, right, DIMS, preferred_element_type=jnp.float32)
                for out, part, first in (
                    (kept[group], value[:cells], group),
                    (sent[group], value[cells:], groups + group),
                ):
                    if before:
                        part = part + before[first][rows, :width]
                    out[rows, :width] = part


def multiply(core, sources, pieces, before=()):
    share, cells, depth = sources[1].shape
    slabs = len(pieces)
    groups = -(-slabs * cells // LANES)
    flops = 2 * share * 2 * cells * slabs * cells * depth
    flat = [part for piece in pieces for part in piece]
    counts = [len(sources[0])] + [len(piece) for piece in pieces]
    return pl.pallas_call(
        functools.partial(multiply_body, counts),
        in_specs=[SCALARS] + [WHOLE] * (1 + sum(counts) + len(before)),
        out_specs=[WHOLE] * (2 * groups),
        out_shape=[jax.ShapeDtypeStruct((share * cells, LANES), jnp.float32)] * (2 * groups),
        scratch_shapes=[pltpu.VMEM((slabs, share, cells, depth), sources[1].dtype)],
        compiler_params=params(),
        cost_estimate=pl.CostEstimate(flops=flops, bytes_accessed=6 << 20, transcendentals=0),
        name="multiply",
    )(core.reshape(1), *in_vmem(*sources[0], sources[1], *flat, *before))


def gather_rows(where_ref, cells, kept_ref, came_ref, rows_ref):
    share = kept_ref.shape[0] // cells
    for ref, first in ((kept_ref, where_ref[6] * share), (came_ref, (1 - where_ref[6]) * share)):
        for place in range(share):
            base = (first + place) * apart(cells)
            rows_ref[pl.ds(base, cells, stride=GAP), :] = ref[place * cells : (place + 1) * cells, :]


def spread_rows(where_ref, cells, slabs, factor, rows_ref, skewed_ref):
    line = skewed_ref.shape[0] // cells
    for cell in range(cells):
        turned = rows_ref[pl.ds(GAP * cell, LANES, stride=apart(cells)), :].T * factor
        for place, slab in enumerate(slabs):
            base = cell * line + GAP * ((where_ref[slab] + 4) * cells - cell)
            skewed_ref[pl.ds(base, cells, stride=GAP), :] = turned[cells * place : cells * (place + 1)]


def write_lags(first, skewed_ref, image_ref, buffer_ref, sems):
    cells = image_ref.shape[1]
    line = skewed_ref.shape[0] // cells
    parts, lags = sems.shape[0], buffer_ref.shape[0]
    cuts = [lags * part // parts for part in range(parts + 1)]
    copies = []
    for part, (start, stop) in enumerate(zip(cuts, cuts[1:])):
        for lag in range(start, stop):
            buffer_ref[lag] = skewed_ref[pl.ds(GAP * (2 * cells + first + lag), cells, stride=line), :]
        source, target = pl.ds(start, stop - start), pl.ds(first + start, stop - start)
        copies.append(pltpu.make_async_copy(buffer_ref.at[source], image_ref.at[target], sems.at[part]))
        copies[-1].start()
    for copy in copies:
        copy.wait()


def early_spread_body(scale, cells, where_ref, kept_ref, came_ref, skewed_ref, image_ref, rows_ref, buffer_ref, sems):
    gather_rows(where_ref, cells, kept_ref, came_ref, rows_ref)
    spread_rows(where_ref, cells, range(4), scale, rows_ref, skewed_ref)
    write_lags(where_ref[7] * 2 * cells, skewed_ref, image_ref, buffer_ref, sems)


def spread_scratch(cells, lags):
    return [
        pltpu.VMEM((LANES * apart(cells), LANES), jnp.float32),
        pltpu.VMEM((lags, cells, LANES), jnp.float32),
        pltpu.SemaphoreType.DMA((2,)),
    ]


def early_spread(scale, cells, where, products):
    lags = 4 * cells + 1
    return pl.pallas_call(
        functools.partial(early_spread_body, scale, cells),
        in_specs=[SCALARS] + [WHOLE] * 2,
        out_specs=[WHOLE, pl.BlockSpec(memory_space=pl.ANY)],
        out_shape=[
            jax.ShapeDtypeStruct((apart(lags + 4 * cells) * cells, LANES), jnp.float32),
            pltpu.HBM((lags, cells, LANES), jnp.float32),
        ],
        scratch_shapes=spread_scratch(cells, 2 * cells + 1),
        compiler_params=params(),
        cost_estimate=pl.CostEstimate(flops=0, bytes_accessed=6 << 20, transcendentals=0),
        name="early_spread",
    )(where, *in_vmem(*products))


def late_spread_body(scale, cells, where_ref, kept_ref, came_ref, _, __, skewed_ref, image_ref, rows_ref, buffer_ref, sems):
    gather_rows(where_ref, cells, kept_ref, came_ref, rows_ref)
    spread_rows(where_ref, cells, (4, 5), scale, rows_ref, skewed_ref)
    write_lags((1 - where_ref[7]) * (2 * cells + 1), skewed_ref, image_ref, buffer_ref, sems)


def late_spread(scale, cells, where, products, skewed, image):
    return pl.pallas_call(
        functools.partial(late_spread_body, scale, cells),
        in_specs=[SCALARS] + [WHOLE] * 3 + [pl.BlockSpec(memory_space=pl.ANY)],
        out_specs=[WHOLE, pl.BlockSpec(memory_space=pl.ANY)],
        out_shape=[jax.ShapeDtypeStruct(skewed.shape, jnp.float32), pltpu.HBM(image.shape, jnp.float32)],
        input_output_aliases={3: 0, 4: 1},
        scratch_shapes=spread_scratch(cells, 2 * cells),
        compiler_params=params(),
        name="late_spread",
    )(where, *in_vmem(*products, skewed), image)[1]


def routed(source, receiver, scale):
    count = lax.axis_size("inline")
    cells = source.shape[1]
    own = lax.axis_index("inline")
    core, odd = own & 1, (own >> 1) & 1
    half = lax.axis_index("shot")

    def across(value):
        return lax.ppermute(value, "shot", [(0, 1), (1, 0)])

    def along_y(value):
        return lax.ppermute(value, "inline", [(index, index ^ 2) for index in range(count)])

    def along_z(value):
        pairs = [(index, index + (4, -4)[index // 2 % 2]) for index in range(count)]
        return lax.ppermute(value, "inline", [pair for pair in pairs if 0 <= pair[1] < count])

    def to_core(value):
        return lax.ppermute(value, "inline", [(index, index ^ 1) for index in range(count)])

    def across_to_core(value):
        pairs = [(2 * index + side, 2 * (index ^ 1) + 1 - side) for index in range(count) for side in range(2)]
        return lax.ppermute(value, ("inline", "shot"), pairs)

    def barrier(*values):
        return lax.optimization_barrier(values)

    which = jnp.stack([half, core]).astype(jnp.int32)
    kept, lent, there, there_twin = turn(receiver, which)
    y0 = along_y(kept)
    twin = to_core(lent)
    there, there_twin, twin = barrier(there, there_twin, twin)
    moved, moved_twin = across(there), across_to_core(there_twin)
    y1 = along_y(twin)
    source, _ = barrier(source, twin)
    left, left_lent, far, far_lent = turn(source, which)
    y0, left = barrier(y0, left)
    y2, z0 = along_y(moved), along_z(y0)
    moved_twin, y1, far, left_lent = barrier(moved_twin, y1, far, left_lent)
    y3, z1 = along_y(moved_twin), along_z(y1)
    left_twin = to_core(left_lent)
    right = across(far)
    z0, far_lent, y2 = barrier(z0, far_lent, y2)
    right_twin = across_to_core(far_lent)
    left_twin, right = barrier(left_twin, right)
    z2 = along_z(y2)
    early = multiply(core, ([left], left_twin), [(piece,) for piece in (kept, twin, y0, y1, z0, z1)])
    y3, *early = barrier(y3, *early)
    z3 = along_z(y3)
    middle = multiply(core, ([right], right_twin), ((moved,), (moved_twin,), (y2,), (y3,)), (early[0], early[2]))
    middle_came = to_core(middle[1])
    side = 2 - 4 * odd
    where = jnp.stack([block + shift - core for shift in (0, side, -side) for block in (0, 1)] + [core, 1 - odd])
    where = where.astype(jnp.int32)
    skewed, image = early_spread(scale, cells, where, (middle[0], middle_came))
    late = multiply(core, ([right], right_twin), ((z2,), (z3,)), (early[1], early[3]))
    late_came = to_core(late[1])
    return late_spread(scale, cells, where, (late[0], late_came), skewed, image)


def on_device(source, receiver):
    shots, cells, times, cross = source.shape
    groups, count = lax.axis_size("shot"), lax.axis_size("inline")
    scale = 1.0 / (times * shots * groups) ** 0.5
    fits = (
        groups == 2
        and count % 4 == 0
        and cross == 2 * LANES
        and shots * times == LANES
        and 4 * cells == LANES
        and times % ROWS == 0
    )
    return routed(source, receiver, scale) if fits else plain(source, receiver, scale)


def solution(mesh):
    placed = (P("shot", "inline", None, None), P("shot", "inline", None, None))
    return jax.shard_map(
        on_device, mesh=mesh, in_specs=placed, out_specs=P(None, "inline", "shot"), check_vma=False
    )
```

```python
import functools

import jax
import jax.numpy as jnp
from jax import lax
from jax.experimental import pallas as pl
from jax.experimental.pallas import tpu as pltpu
from jax.sharding import PartitionSpec as P

LANES = 128
ROWS = 16
VMEM_BYTES = 24 * 1024 * 1024


def shifted(value, axis, steps):
    count = lax.axis_size(axis)
    initial, last = (max(0, -steps), min(count, count - steps))
    return lax.ppermute(value, axis, [(source, source + steps) for source in range(initial, last)])


def band_rows(product, width, lags):
    rows = product.shape[0]
    cross = product.shape[2]
    flat = product.reshape(rows * width, cross)
    flat = jnp.pad(flat, ((0, rows), (0, 0)))
    skewed = flat.reshape(rows, width + 1, cross)[:, :lags, :]
    return jnp.transpose(skewed, (1, 0, 2))


def plain(source, receiver, scale):
    source, receiver = (
        lax.all_to_all(value, "shot", split_axis=3, concat_axis=0, tiled=True) for value in (source, receiver)
    )
    cells = source.shape[1]
    slabs = [receiver if step == 0 else shifted(receiver, "inline", -step) for step in (-2, -1, 0, 1, 2)]
    width = 5 * cells
    product = jnp.einsum(
        "sity,szty->izy", source, jnp.concatenate(slabs, axis=1), preferred_element_type=jnp.float32
    )
    return band_rows(product, width, 4 * cells + 1) * scale


GAP = 3


def apart(count):
    stride = GAP * count
    return stride + 1 - stride % 2


def in_vmem(*values):
    return [pltpu.with_memory_space_constraint(value, pltpu.VMEM) for value in values]


def params():
    return pltpu.CompilerParams(vmem_limit_bytes=VMEM_BYTES)


SCALARS = pl.BlockSpec(memory_space=pltpu.SMEM)
WHOLE = pl.BlockSpec(memory_space=pltpu.VMEM)


def turn_body(which_ref, raw_ref, *refs):
    turned_refs, (buffer_ref, rows_ref, sems) = refs[:4], refs[4:]
    parts, shots, count, times, cross = buffer_ref.shape
    cells = parts * count
    copies = [
        pltpu.make_async_copy(raw_ref.at[:, pl.ds(part * count, count)], buffer_ref.at[part], sems.at[part])
        for part in range(parts)
    ]
    for copy in copies:
        copy.start()
    for part, copy in enumerate(copies):
        copy.wait()
        for cell in range(count):
            for lanes in range(0, cross, LANES):
                tile = buffer_ref[part, :, cell, :, lanes : lanes + LANES].reshape(shots * times, LANES)
                base = lanes * apart(cells) + GAP * (part * count + cell)
                rows_ref[pl.ds(base, LANES, stride=apart(cells)), :] = tile.astype(jnp.float32).T
    half, core = which_ref[0], which_ref[1]
    quarters = [2 * half + core, 2 * half + 1 - core, 2 - 2 * half + core, 3 - 2 * half - core]
    for turned_ref, quarter in zip(turned_refs, quarters):
        share = turned_ref.shape[0]
        for place in range(share):
            base = (quarter * share + place) * apart(cells)
            turned_ref[place] = rows_ref[pl.ds(base, cells, stride=GAP), :].astype(turned_ref.dtype)


def turn(raw, which):
    shots, cells, times, cross = raw.shape
    depth = shots * times
    chunks = 4
    return pl.pallas_call(
        turn_body,
        in_specs=[SCALARS, pl.BlockSpec(memory_space=pl.ANY)],
        out_specs=[WHOLE] * 4,
        out_shape=[jax.ShapeDtypeStruct((cross // 4, cells, depth), raw.dtype)] * 4,
        scratch_shapes=[
            pltpu.VMEM((chunks, shots, cells // chunks, times, cross), raw.dtype),
            pltpu.VMEM((cross * apart(cells), depth), jnp.float32),
            pltpu.SemaphoreType.DMA((chunks,)),
        ],
        compiler_params=params(),
        cost_estimate=pl.CostEstimate(flops=0, bytes_accessed=raw.size * 4, transcendentals=0),
        name="turn",
    )(which, pltpu.with_memory_space_constraint(raw, pltpu.HBM))


DIMS = (((1,), (1,)), ((), ()))


def multiply_body(pieces, core_ref, *refs):
    own, *pieces = pieces
    slabs = len(pieces)
    sources, right_ref = (refs[:own], refs[own]), refs[-1]
    ins = refs[own + 1 : own + 1 + sum(pieces)]
    share, cells, _ = refs[own].shape
    groups = (slabs * cells + LANES - 1) // LANES
    kept, sent = refs[-1 - 2 * groups : -1 - groups], refs[-1 - groups : -1]
    before = refs[own + 1 + len(ins) : -1 - 2 * groups]
    for place, count in enumerate(pieces):
        side, other = divmod(place, 2)
        slab = 2 * side + (core_ref[0] if other == 0 else 1 - core_ref[0])
        for part in range(count):
            right_ref[slab, part * (share // count) : (part + 1) * (share // count)] = ins[part][...]
        ins = ins[count:]

    for cross_part in range(own):
        first_cross = cross_part * (share // own)
        for place in range(share // own):
            cross = first_cross + place
            left = jnp.concatenate([sources[0][cross_part][place], sources[1][cross]], axis=0)
            rows = pl.ds(cross * cells, cells)
            for group in range(groups):
                members = range(group * LANES // cells, min(slabs, (group + 1) * LANES // cells))
                right = jnp.concatenate([right_ref[slab, cross] for slab in members], axis=0)
                width = len(members) * cells
                value = lax.dot_general(left, right, DIMS, preferred_element_type=jnp.float32)
                for out, part, first in (
                    (kept[group], value[:cells], group),
                    (sent[group], value[cells:], groups + group),
                ):
                    if before:
                        part = part + before[first][rows, :width]
                    out[rows, :width] = part


def multiply(core, sources, pieces, before=()):
    share, cells, depth = sources[1].shape
    slabs = len(pieces)
    groups = -(-slabs * cells // LANES)
    flops = 2 * share * 2 * cells * slabs * cells * depth
    flat = [part for piece in pieces for part in piece]
    counts = [len(sources[0])] + [len(piece) for piece in pieces]
    return pl.pallas_call(
        functools.partial(multiply_body, counts),
        in_specs=[SCALARS] + [WHOLE] * (1 + sum(counts) + len(before)),
        out_specs=[WHOLE] * (2 * groups),
        out_shape=[jax.ShapeDtypeStruct((share * cells, LANES), jnp.float32)] * (2 * groups),
        scratch_shapes=[pltpu.VMEM((slabs, share, cells, depth), sources[1].dtype)],
        compiler_params=params(),
        cost_estimate=pl.CostEstimate(flops=flops, bytes_accessed=6 << 20, transcendentals=0),
        name="multiply",
    )(core.reshape(1), *in_vmem(*sources[0], sources[1], *flat, *before))


def gather_rows(where_ref, cells, kept_ref, came_ref, rows_ref):
    share = kept_ref.shape[0] // cells
    for ref, first in ((kept_ref, where_ref[6] * share), (came_ref, (1 - where_ref[6]) * share)):
        for place in range(share):
            base = (first + place) * apart(cells)
            rows_ref[pl.ds(base, cells, stride=GAP), :] = ref[place * cells : (place + 1) * cells, :]


def spread_rows(where_ref, cells, slabs, factor, rows_ref, skewed_ref):
    line = skewed_ref.shape[0] // cells
    for cell in range(cells):
        turned = rows_ref[pl.ds(GAP * cell, LANES, stride=apart(cells)), :].T * factor
        for place, slab in enumerate(slabs):
            base = cell * line + GAP * ((where_ref[slab] + 4) * cells - cell)
            skewed_ref[pl.ds(base, cells, stride=GAP), :] = turned[cells * place : cells * (place + 1)]


def early_spread_body(scale, cells, where_ref, kept_ref, came_ref, skewed_ref, rows_ref):
    gather_rows(where_ref, cells, kept_ref, came_ref, rows_ref)
    spread_rows(where_ref, cells, range(4), scale, rows_ref, skewed_ref)


def early_spread(scale, cells, where, products):
    rows = apart(4 * cells + 1 + 4 * cells) * cells
    return pl.pallas_call(
        functools.partial(early_spread_body, scale, cells),
        in_specs=[SCALARS] + [WHOLE] * 2,
        out_specs=WHOLE,
        out_shape=jax.ShapeDtypeStruct((rows, LANES), jnp.float32),
        scratch_shapes=[pltpu.VMEM((LANES * apart(cells), LANES), jnp.float32)],
        compiler_params=params(),
        cost_estimate=pl.CostEstimate(flops=0, bytes_accessed=6 << 20, transcendentals=0),
        name="early_spread",
    )(where, *in_vmem(*products))


def late_spread_body(scale, cells, where_ref, kept_ref, came_ref, _, skewed_ref, image_ref, rows_ref, buffer_ref, sems):
    line = skewed_ref.shape[0] // cells
    side = 2 * cells

    def send(first, count, sem):
        for lag in range(count):
            row = GAP * (2 * cells + first + lag)
            buffer_ref[first + lag] = skewed_ref[pl.ds(row, cells, stride=line), :]
        block = pl.ds(first, count)
        copy = pltpu.make_async_copy(buffer_ref.at[block], image_ref.at[block], sem)
        copy.start()
        return copy

    copies = [send(where_ref[7] * side, side + 1, sems.at[0])]
    gather_rows(where_ref, cells, kept_ref, came_ref, rows_ref)
    spread_rows(where_ref, cells, (4, 5), scale, rows_ref, skewed_ref)
    for part in range(2):
        first = (1 - where_ref[7]) * (side + 1) + part * (side // 2)
        copies.append(send(first, side // 2, sems.at[1 + part]))
    for copy in copies:
        copy.wait()


def late_spread(scale, cells, where, products, skewed):
    lags = 4 * cells + 1
    return pl.pallas_call(
        functools.partial(late_spread_body, scale, cells),
        in_specs=[SCALARS] + [WHOLE] * 3,
        out_specs=[WHOLE, pl.BlockSpec(memory_space=pl.ANY)],
        out_shape=[
            jax.ShapeDtypeStruct(skewed.shape, jnp.float32),
            jax.ShapeDtypeStruct((lags, cells, LANES), jnp.float32),
        ],
        input_output_aliases={3: 0},
        scratch_shapes=[
            pltpu.VMEM((LANES * apart(cells), LANES), jnp.float32),
            pltpu.VMEM((lags, cells, LANES), jnp.float32),
            pltpu.SemaphoreType.DMA((3,)),
        ],
        compiler_params=params(),
        name="late_spread",
    )(where, *in_vmem(*products, skewed))[1]


def routed(source, receiver, scale):
    count = lax.axis_size("inline")
    cells = source.shape[1]
    own = lax.axis_index("inline")
    core, odd = own & 1, (own >> 1) & 1
    half = lax.axis_index("shot")

    def across(value):
        return lax.ppermute(value, "shot", [(0, 1), (1, 0)])

    def along_y(value):
        return lax.ppermute(value, "inline", [(index, index ^ 2) for index in range(count)])

    def along_z(value):
        pairs = [(index, index + (4, -4)[index // 2 % 2]) for index in range(count)]
        return lax.ppermute(value, "inline", [pair for pair in pairs if 0 <= pair[1] < count])

    def to_core(value):
        return lax.ppermute(value, "inline", [(index, index ^ 1) for index in range(count)])

    def across_to_core(value):
        pairs = [(2 * index + side, 2 * (index ^ 1) + 1 - side) for index in range(count) for side in range(2)]
        return lax.ppermute(value, ("inline", "shot"), pairs)

    def barrier(*values):
        return lax.optimization_barrier(values)

    which = jnp.stack([half, core]).astype(jnp.int32)
    kept, lent, there, there_twin = turn(receiver, which)
    y0 = along_y(kept)
    twin = to_core(lent)
    there, there_twin, twin = barrier(there, there_twin, twin)
    moved, moved_twin = across(there), across_to_core(there_twin)
    y1 = along_y(twin)
    source, _ = barrier(source, twin)
    left, left_lent, far, far_lent = turn(source, which)
    y0, left = barrier(y0, left)
    y2, z0 = along_y(moved), along_z(y0)
    moved_twin, y1, far, left_lent = barrier(moved_twin, y1, far, left_lent)
    y3, z1 = along_y(moved_twin), along_z(y1)
    left_twin = to_core(left_lent)
    right = across(far)
    z0, far_lent, y2 = barrier(z0, far_lent, y2)
    right_twin = across_to_core(far_lent)
    left_twin, right = barrier(left_twin, right)
    z2 = along_z(y2)
    y3, z1 = barrier(y3, z1)
    z3 = along_z(y3)
    left_twin, y3, z2 = barrier(left_twin, y3, z2)
    early = multiply(core, ([left], left_twin), [(piece,) for piece in (kept, twin, y0, y1, z0, z1)])
    middle = multiply(core, ([right], right_twin), ((moved,), (moved_twin,), (y2,), (y3,)), (early[0], early[2]))
    middle_came = to_core(middle[1])
    side = 2 - 4 * odd
    where = jnp.stack([block + shift - core for shift in (0, side, -side) for block in (0, 1)] + [core, 1 - odd])
    where = where.astype(jnp.int32)
    skewed = early_spread(scale, cells, where, (middle[0], middle_came))
    late = multiply(core, ([right], right_twin), ((z2,), (z3,)), (early[1], early[3]))
    late_came = to_core(late[1])
    return late_spread(scale, cells, where, (late[0], late_came), skewed)


def on_device(source, receiver):
    shots, cells, times, cross = source.shape
    groups, count = lax.axis_size("shot"), lax.axis_size("inline")
    scale = 1.0 / (times * shots * groups) ** 0.5
    fits = (
        groups == 2
        and count % 4 == 0
        and cross == 2 * LANES
        and shots * times == LANES
        and 4 * cells == LANES
        and times % ROWS == 0
    )
    return routed(source, receiver, scale) if fits else plain(source, receiver, scale)


def solution(mesh):
    placed = (P("shot", "inline", None, None), P("shot", "inline", None, None))
    return jax.shard_map(
        on_device, mesh=mesh, in_specs=placed, out_specs=P(None, "inline", "shot"), check_vma=False
    )
```

```python
import functools

import jax
import jax.numpy as jnp
from jax import lax
from jax.experimental import pallas as pl
from jax.experimental.pallas import tpu as pltpu
from jax.sharding import PartitionSpec as P

LANES = 128
ROWS = 16
VMEM_BYTES = 24 * 1024 * 1024


def shifted(value, axis, steps):
    count = lax.axis_size(axis)
    initial, last = (max(0, -steps), min(count, count - steps))
    return lax.ppermute(value, axis, [(source, source + steps) for source in range(initial, last)])


def band_rows(product, width, lags):
    rows = product.shape[0]
    cross = product.shape[2]
    flat = product.reshape(rows * width, cross)
    flat = jnp.pad(flat, ((0, rows), (0, 0)))
    skewed = flat.reshape(rows, width + 1, cross)[:, :lags, :]
    return jnp.transpose(skewed, (1, 0, 2))


def plain(source, receiver, scale):
    source, receiver = (
        lax.all_to_all(value, "shot", split_axis=3, concat_axis=0, tiled=True) for value in (source, receiver)
    )
    cells = source.shape[1]
    slabs = [receiver if step == 0 else shifted(receiver, "inline", -step) for step in (-2, -1, 0, 1, 2)]
    width = 5 * cells
    product = jnp.einsum(
        "sity,szty->izy", source, jnp.concatenate(slabs, axis=1), preferred_element_type=jnp.float32
    )
    return band_rows(product, width, 4 * cells + 1) * scale


GAP = 3


def apart(count):
    stride = GAP * count
    return stride + 1 - stride % 2


def in_vmem(*values):
    return [pltpu.with_memory_space_constraint(value, pltpu.VMEM) for value in values]


def params():
    return pltpu.CompilerParams(vmem_limit_bytes=VMEM_BYTES)


SCALARS = pl.BlockSpec(memory_space=pltpu.SMEM)
WHOLE = pl.BlockSpec(memory_space=pltpu.VMEM)


def turn_body(which_ref, raw_ref, own_ref, other_ref, buffer_ref, rows_ref, sems):
    chunks, shots, count, times, cross = buffer_ref.shape
    cells = chunks * count
    lanes = pl.ds(pl.multiple_of(which_ref[0] * cross, cross), cross)
    copies = [
        pltpu.make_async_copy(
            raw_ref.at[:, pl.ds(chunk * count, count), :, lanes], buffer_ref.at[chunk], sems.at[chunk]
        )
        for chunk in range(chunks)
    ]
    for copy in copies:
        copy.start()
    for chunk, copy in enumerate(copies):
        copy.wait()
        for cell in range(count):
            tile = buffer_ref[chunk, :, cell].reshape(shots * times, cross).astype(jnp.float32)
            rows_ref[pl.ds(GAP * (chunk * count + cell), cross, stride=apart(cells)), :] = tile.T
    share = cross // 2
    for turned_ref, part in ((own_ref, which_ref[1]), (other_ref, 1 - which_ref[1])):
        for place in range(share):
            base = (part * share + place) * apart(cells)
            turned_ref[place] = rows_ref[pl.ds(base, cells, stride=GAP), :].astype(turned_ref.dtype)


def turn(raw, half, core):
    shots, cells, times, _ = raw.shape
    depth = shots * times
    chunks = 4
    return pl.pallas_call(
        turn_body,
        in_specs=[SCALARS, pl.BlockSpec(memory_space=pl.ANY)],
        out_specs=[WHOLE] * 2,
        out_shape=[jax.ShapeDtypeStruct((LANES // 2, cells, depth), raw.dtype)] * 2,
        scratch_shapes=[
            pltpu.VMEM((chunks, shots, cells // chunks, times, LANES), raw.dtype),
            pltpu.VMEM((LANES * apart(cells), depth), jnp.float32),
            pltpu.SemaphoreType.DMA((chunks,)),
        ],
        compiler_params=params(),
        cost_estimate=pl.CostEstimate(flops=0, bytes_accessed=raw.size * 2, transcendentals=0),
        name="turn",
    )(jnp.stack([half, core]).astype(jnp.int32), pltpu.with_memory_space_constraint(raw, pltpu.HBM))


DIMS = (((1,), (1,)), ((), ()))


def multiply_body(pieces, core_ref, *refs):
    own, *pieces = pieces
    slabs = len(pieces)
    sources, right_ref = (refs[:own], refs[own]), refs[-1]
    ins = refs[own + 1 : own + 1 + sum(pieces)]
    share, cells, _ = refs[own].shape
    groups = (slabs * cells + LANES - 1) // LANES
    kept, sent = refs[-1 - 2 * groups : -1 - groups], refs[-1 - groups : -1]
    before = refs[own + 1 + len(ins) : -1 - 2 * groups]
    for place, count in enumerate(pieces):
        side, other = divmod(place, 2)
        slab = 2 * side + (core_ref[0] if other == 0 else 1 - core_ref[0])
        for part in range(count):
            right_ref[slab, part * (share // count) : (part + 1) * (share // count)] = ins[part][...]
        ins = ins[count:]

    for cross_part in range(own):
        first_cross = cross_part * (share // own)
        for place in range(share // own):
            cross = first_cross + place
            left = jnp.concatenate([sources[0][cross_part][place], sources[1][cross]], axis=0)
            rows = pl.ds(cross * cells, cells)
            for group in range(groups):
                members = range(group * LANES // cells, min(slabs, (group + 1) * LANES // cells))
                right = jnp.concatenate([right_ref[slab, cross] for slab in members], axis=0)
                width = len(members) * cells
                value = lax.dot_general(left, right, DIMS, preferred_element_type=jnp.float32)
                for out, part, first in (
                    (kept[group], value[:cells], group),
                    (sent[group], value[cells:], groups + group),
                ):
                    if before:
                        part = part + before[first][rows, :width]
                    out[rows, :width] = part


def multiply(core, sources, pieces, before=()):
    share, cells, depth = sources[1].shape
    slabs = len(pieces)
    groups = -(-slabs * cells // LANES)
    flops = 2 * share * 2 * cells * slabs * cells * depth
    flat = [part for piece in pieces for part in piece]
    counts = [len(sources[0])] + [len(piece) for piece in pieces]
    return pl.pallas_call(
        functools.partial(multiply_body, counts),
        in_specs=[SCALARS] + [WHOLE] * (1 + sum(counts) + len(before)),
        out_specs=[WHOLE] * (2 * groups),
        out_shape=[jax.ShapeDtypeStruct((share * cells, LANES), jnp.float32)] * (2 * groups),
        scratch_shapes=[pltpu.VMEM((slabs, share, cells, depth), sources[1].dtype)],
        compiler_params=params(),
        cost_estimate=pl.CostEstimate(flops=flops, bytes_accessed=6 << 20, transcendentals=0),
        name="multiply",
    )(core.reshape(1), *in_vmem(*sources[0], sources[1], *flat, *before))


def gather_rows(where_ref, cells, kept_ref, came_ref, rows_ref):
    share = kept_ref.shape[0] // cells
    for ref, first in ((kept_ref, where_ref[6] * share), (came_ref, (1 - where_ref[6]) * share)):
        for place in range(share):
            base = (first + place) * apart(cells)
            rows_ref[pl.ds(base, cells, stride=GAP), :] = ref[place * cells : (place + 1) * cells, :]


def spread_rows(where_ref, cells, slabs, factor, rows_ref, skewed_ref):
    line = skewed_ref.shape[0] // cells
    for cell in range(cells):
        turned = rows_ref[pl.ds(GAP * cell, LANES, stride=apart(cells)), :].T * factor
        for place, slab in enumerate(slabs):
            base = cell * line + GAP * ((where_ref[slab] + 4) * cells - cell)
            skewed_ref[pl.ds(base, cells, stride=GAP), :] = turned[cells * place : cells * (place + 1)]


def write_lags(first, skewed_ref, image_ref, buffer_ref, sems):
    cells = image_ref.shape[1]
    line = skewed_ref.shape[0] // cells
    parts, lags = sems.shape[0], buffer_ref.shape[0]
    cuts = [lags * part // parts for part in range(parts + 1)]
    copies = []
    for part, (start, stop) in enumerate(zip(cuts, cuts[1:])):
        for lag in range(start, stop):
            buffer_ref[lag] = skewed_ref[pl.ds(GAP * (2 * cells + first + lag), cells, stride=line), :]
        source, target = pl.ds(start, stop - start), pl.ds(first + start, stop - start)
        copies.append(pltpu.make_async_copy(buffer_ref.at[source], image_ref.at[target], sems.at[part]))
        copies[-1].start()
    for copy in copies:
        copy.wait()


def early_spread_body(scale, cells, where_ref, kept_ref, came_ref, skewed_ref, image_ref, rows_ref, buffer_ref, sems):
    gather_rows(where_ref, cells, kept_ref, came_ref, rows_ref)
    spread_rows(where_ref, cells, range(4), scale, rows_ref, skewed_ref)
    write_lags(where_ref[7] * 2 * cells, skewed_ref, image_ref, buffer_ref, sems)


def spread_scratch(cells, lags):
    return [
        pltpu.VMEM((LANES * apart(cells), LANES), jnp.float32),
        pltpu.VMEM((lags, cells, LANES), jnp.float32),
        pltpu.SemaphoreType.DMA((2,)),
    ]


def early_spread(scale, cells, where, products):
    lags = 4 * cells + 1
    return pl.pallas_call(
        functools.partial(early_spread_body, scale, cells),
        in_specs=[SCALARS] + [WHOLE] * 2,
        out_specs=[WHOLE, pl.BlockSpec(memory_space=pl.ANY)],
        out_shape=[
            jax.ShapeDtypeStruct((apart(lags + 4 * cells) * cells, LANES), jnp.float32),
            pltpu.HBM((lags, cells, LANES), jnp.float32),
        ],
        scratch_shapes=spread_scratch(cells, 2 * cells + 1),
        compiler_params=params(),
        cost_estimate=pl.CostEstimate(flops=0, bytes_accessed=6 << 20, transcendentals=0),
        name="early_spread",
    )(where, *in_vmem(*products))


def late_spread_body(scale, cells, where_ref, kept_ref, came_ref, _, __, skewed_ref, image_ref, rows_ref, buffer_ref, sems):
    gather_rows(where_ref, cells, kept_ref, came_ref, rows_ref)
    spread_rows(where_ref, cells, (4, 5), scale, rows_ref, skewed_ref)
    write_lags((1 - where_ref[7]) * (2 * cells + 1), skewed_ref, image_ref, buffer_ref, sems)


def late_spread(scale, cells, where, products, skewed, image):
    return pl.pallas_call(
        functools.partial(late_spread_body, scale, cells),
        in_specs=[SCALARS] + [WHOLE] * 3 + [pl.BlockSpec(memory_space=pl.ANY)],
        out_specs=[WHOLE, pl.BlockSpec(memory_space=pl.ANY)],
        out_shape=[jax.ShapeDtypeStruct(skewed.shape, jnp.float32), pltpu.HBM(image.shape, jnp.float32)],
        input_output_aliases={3: 0, 4: 1},
        scratch_shapes=spread_scratch(cells, 2 * cells),
        compiler_params=params(),
        name="late_spread",
    )(where, *in_vmem(*products, skewed), image)[1]


def routed(source, receiver, scale):
    count = lax.axis_size("inline")
    cells = source.shape[1]
    own = lax.axis_index("inline")
    core, odd = own & 1, (own >> 1) & 1
    half = lax.axis_index("shot")

    def across(value):
        return lax.ppermute(value, "shot", [(0, 1), (1, 0)])

    def along_y(value):
        return lax.ppermute(value, "inline", [(index, index ^ 2) for index in range(count)])

    def along_z(value):
        pairs = [(index, index + (4, -4)[index // 2 % 2]) for index in range(count)]
        return lax.ppermute(value, "inline", [pair for pair in pairs if 0 <= pair[1] < count])

    def to_core(value):
        return lax.ppermute(value, "inline", [(index, index ^ 1) for index in range(count)])

    def across_to_core(value):
        pairs = [(2 * index + side, 2 * (index ^ 1) + 1 - side) for index in range(count) for side in range(2)]
        return lax.ppermute(value, ("inline", "shot"), pairs)

    def barrier(*values):
        return lax.optimization_barrier(values)

    receiver0, source0 = receiver, source
    side = 2 - 4 * odd
    where = jnp.stack([block + shift - core for shift in (0, side, -side) for block in (0, 1)] + [core, 1 - odd])
    where = where.astype(jnp.int32)
    kept, lent = turn(receiver0, half, core)
    y0 = along_y(kept)
    twin = to_core(lent)
    receiver_tied, *_ = barrier(receiver0, kept)
    there, there_twin = turn(receiver_tied, 1 - half, core)
    there_tied, *_ = barrier(there, twin)
    moved = across(there_tied)
    there_twin_tied, *_ = barrier(there_twin, twin)
    moved_twin = across_to_core(there_twin_tied)
    source_tied, *_ = barrier(source0, there)
    left, left_lent = turn(source_tied, half, core)
    source2_tied, *_ = barrier(source0, left)
    far, far_lent = turn(source2_tied, 1 - half, core)
    y1 = along_y(twin)
    y2 = along_y(moved)
    moved_twin_tied, *_ = barrier(moved_twin, y1)
    y3 = along_y(moved_twin_tied)
    y0_tied, *_ = barrier(y0, left)
    z0 = along_z(y0_tied)
    z1 = along_z(y1)
    left_lent_tied, *_ = barrier(left_lent, moved_twin)
    left_twin = to_core(left_lent_tied)
    far_tied, *_ = barrier(far, y1)
    right = across(far_tied)
    far_lent_tied, *_ = barrier(far_lent, y2)
    right_twin = across_to_core(far_lent_tied)
    y2_tied, *_ = barrier(y2, z0)
    z2 = along_z(y2_tied)
    left_twin_tied, *_ = barrier(left_twin, right)
    early = multiply(core, ([left], left_twin_tied), [(piece,) for piece in (kept, twin, y0, y1, z0, z1)])
    y3_tied, *_ = barrier(y3, z1)
    z3 = along_z(y3_tied)
    right_twin_tied, *_ = barrier(right_twin, z2)
    middle = multiply(core, ([right], right_twin_tied), ((moved,), (moved_twin,), (y2,), (y3,)), (early[0], early[2]))
    middle_came = to_core(middle[1])
    skewed, image = early_spread(scale, cells, where, (middle[0], middle_came))
    late = multiply(core, ([right], right_twin), ((z2,), (z3,)), (early[1], early[3]))
    late_came = to_core(late[1])
    return late_spread(scale, cells, where, (late[0], late_came), skewed, image)


def on_device(source, receiver):
    shots, cells, times, cross = source.shape
    groups, count = lax.axis_size("shot"), lax.axis_size("inline")
    scale = 1.0 / (times * shots * groups) ** 0.5
    fits = (
        groups == 2
        and count % 4 == 0
        and cross == 2 * LANES
        and shots * times == LANES
        and 4 * cells == LANES
        and times % ROWS == 0
    )
    return routed(source, receiver, scale) if fits else plain(source, receiver, scale)


def solution(mesh):
    placed = (P("shot", "inline", None, None), P("shot", "inline", None, None))
    return jax.shard_map(
        on_device, mesh=mesh, in_specs=placed, out_specs=P(None, "inline", "shot"), check_vma=False
    )
```

```python
import functools

import jax
import jax.numpy as jnp
from jax import lax
from jax.experimental import pallas as pl
from jax.experimental.pallas import tpu as pltpu
from jax.sharding import PartitionSpec as P

LANES = 128
ROWS = 16
VMEM_BYTES = 24 * 1024 * 1024


def shifted(value, axis, steps):
    count = lax.axis_size(axis)
    initial, last = (max(0, -steps), min(count, count - steps))
    return lax.ppermute(value, axis, [(source, source + steps) for source in range(initial, last)])


def band_rows(product, width, lags):
    rows = product.shape[0]
    cross = product.shape[2]
    flat = product.reshape(rows * width, cross)
    flat = jnp.pad(flat, ((0, rows), (0, 0)))
    skewed = flat.reshape(rows, width + 1, cross)[:, :lags, :]
    return jnp.transpose(skewed, (1, 0, 2))


def plain(source, receiver, scale):
    source, receiver = (
        lax.all_to_all(value, "shot", split_axis=3, concat_axis=0, tiled=True) for value in (source, receiver)
    )
    cells = source.shape[1]
    slabs = [receiver if step == 0 else shifted(receiver, "inline", -step) for step in (-2, -1, 0, 1, 2)]
    width = 5 * cells
    product = jnp.einsum(
        "sity,szty->izy", source, jnp.concatenate(slabs, axis=1), preferred_element_type=jnp.float32
    )
    return band_rows(product, width, 4 * cells + 1) * scale


GAP = 3


def apart(count):
    stride = GAP * count
    return stride + 1 - stride % 2


def in_vmem(*values):
    return [pltpu.with_memory_space_constraint(value, pltpu.VMEM) for value in values]


def params():
    return pltpu.CompilerParams(vmem_limit_bytes=VMEM_BYTES)


SCALARS = pl.BlockSpec(memory_space=pltpu.SMEM)
WHOLE = pl.BlockSpec(memory_space=pltpu.VMEM)


def turn_body(which_ref, raw_ref, own_ref, other_ref, buffer_ref, rows_ref, sems):
    chunks, shots, count, times, cross = buffer_ref.shape
    cells = chunks * count
    lanes = pl.ds(pl.multiple_of(which_ref[0] * cross, cross), cross)
    copies = [
        pltpu.make_async_copy(
            raw_ref.at[:, pl.ds(chunk * count, count), :, lanes], buffer_ref.at[chunk], sems.at[chunk]
        )
        for chunk in range(chunks)
    ]
    for copy in copies:
        copy.start()
    for chunk, copy in enumerate(copies):
        copy.wait()
        for cell in range(count):
            tile = buffer_ref[chunk, :, cell].reshape(shots * times, cross).astype(jnp.float32)
            rows_ref[pl.ds(GAP * (chunk * count + cell), cross, stride=apart(cells)), :] = tile.T
    share = cross // 2
    for turned_ref, part in ((own_ref, which_ref[1]), (other_ref, 1 - which_ref[1])):
        for place in range(share):
            base = (part * share + place) * apart(cells)
            turned_ref[place] = rows_ref[pl.ds(base, cells, stride=GAP), :].astype(turned_ref.dtype)


def turn(raw, half, core):
    shots, cells, times, _ = raw.shape
    depth = shots * times
    chunks = 4
    return pl.pallas_call(
        turn_body,
        in_specs=[SCALARS, pl.BlockSpec(memory_space=pl.ANY)],
        out_specs=[WHOLE] * 2,
        out_shape=[jax.ShapeDtypeStruct((LANES // 2, cells, depth), raw.dtype)] * 2,
        scratch_shapes=[
            pltpu.VMEM((chunks, shots, cells // chunks, times, LANES), raw.dtype),
            pltpu.VMEM((LANES * apart(cells), depth), jnp.float32),
            pltpu.SemaphoreType.DMA((chunks,)),
        ],
        compiler_params=params(),
        cost_estimate=pl.CostEstimate(flops=0, bytes_accessed=raw.size * 2, transcendentals=0),
        name="turn",
    )(jnp.stack([half, core]).astype(jnp.int32), pltpu.with_memory_space_constraint(raw, pltpu.HBM))


DIMS = (((1,), (1,)), ((), ()))


def multiply_body(pieces, core_ref, *refs):
    own, *pieces = pieces
    slabs = len(pieces)
    sources, right_ref = (refs[:own], refs[own]), refs[-1]
    ins = refs[own + 1 : own + 1 + sum(pieces)]
    share, cells, _ = refs[own].shape
    groups = (slabs * cells + LANES - 1) // LANES
    kept, sent = refs[-1 - 2 * groups : -1 - groups], refs[-1 - groups : -1]
    before = refs[own + 1 + len(ins) : -1 - 2 * groups]
    for place, count in enumerate(pieces):
        side, other = divmod(place, 2)
        slab = 2 * side + (core_ref[0] if other == 0 else 1 - core_ref[0])
        for part in range(count):
            right_ref[slab, part * (share // count) : (part + 1) * (share // count)] = ins[part][...]
        ins = ins[count:]

    for cross_part in range(own):
        first_cross = cross_part * (share // own)
        for place in range(share // own):
            cross = first_cross + place
            left = jnp.concatenate([sources[0][cross_part][place], sources[1][cross]], axis=0)
            rows = pl.ds(cross * cells, cells)
            for group in range(groups):
                members = range(group * LANES // cells, min(slabs, (group + 1) * LANES // cells))
                right = jnp.concatenate([right_ref[slab, cross] for slab in members], axis=0)
                width = len(members) * cells
                value = lax.dot_general(left, right, DIMS, preferred_element_type=jnp.float32)
                for out, part, first in (
                    (kept[group], value[:cells], group),
                    (sent[group], value[cells:], groups + group),
                ):
                    if before:
                        part = part + before[first][rows, :width]
                    out[rows, :width] = part


def multiply(core, sources, pieces, before=()):
    share, cells, depth = sources[1].shape
    slabs = len(pieces)
    groups = -(-slabs * cells // LANES)
    flops = 2 * share * 2 * cells * slabs * cells * depth
    flat = [part for piece in pieces for part in piece]
    counts = [len(sources[0])] + [len(piece) for piece in pieces]
    return pl.pallas_call(
        functools.partial(multiply_body, counts),
        in_specs=[SCALARS] + [WHOLE] * (1 + sum(counts) + len(before)),
        out_specs=[WHOLE] * (2 * groups),
        out_shape=[jax.ShapeDtypeStruct((share * cells, LANES), jnp.float32)] * (2 * groups),
        scratch_shapes=[pltpu.VMEM((slabs, share, cells, depth), sources[1].dtype)],
        compiler_params=params(),
        cost_estimate=pl.CostEstimate(flops=flops, bytes_accessed=6 << 20, transcendentals=0),
        name="multiply",
    )(core.reshape(1), *in_vmem(*sources[0], sources[1], *flat, *before))


def gather_rows(where_ref, cells, kept_ref, came_ref, rows_ref):
    share = kept_ref.shape[0] // cells
    for ref, first in ((kept_ref, where_ref[6] * share), (came_ref, (1 - where_ref[6]) * share)):
        for place in range(share):
            base = (first + place) * apart(cells)
            rows_ref[pl.ds(base, cells, stride=GAP), :] = ref[place * cells : (place + 1) * cells, :]


def spread_rows(where_ref, cells, slabs, factor, rows_ref, skewed_ref):
    line = skewed_ref.shape[0] // cells
    for cell in range(cells):
        turned = rows_ref[pl.ds(GAP * cell, LANES, stride=apart(cells)), :].T * factor
        for place, slab in enumerate(slabs):
            base = cell * line + GAP * ((where_ref[slab] + 4) * cells - cell)
            skewed_ref[pl.ds(base, cells, stride=GAP), :] = turned[cells * place : cells * (place + 1)]


def write_lags(first, skewed_ref, image_ref, buffer_ref, sems):
    cells = image_ref.shape[1]
    line = skewed_ref.shape[0] // cells
    parts, lags = sems.shape[0], buffer_ref.shape[0]
    cuts = [lags * part // parts for part in range(parts + 1)]
    copies = []
    for part, (start, stop) in enumerate(zip(cuts, cuts[1:])):
        for lag in range(start, stop):
            buffer_ref[lag] = skewed_ref[pl.ds(GAP * (2 * cells + first + lag), cells, stride=line), :]
        source, target = pl.ds(start, stop - start), pl.ds(first + start, stop - start)
        copies.append(pltpu.make_async_copy(buffer_ref.at[source], image_ref.at[target], sems.at[part]))
        copies[-1].start()
    for copy in copies:
        copy.wait()


def early_spread_body(scale, cells, where_ref, kept_ref, came_ref, skewed_ref, image_ref, rows_ref, buffer_ref, sems):
    gather_rows(where_ref, cells, kept_ref, came_ref, rows_ref)
    spread_rows(where_ref, cells, range(4), scale, rows_ref, skewed_ref)
    write_lags(where_ref[7] * 2 * cells, skewed_ref, image_ref, buffer_ref, sems)


def spread_scratch(cells, lags):
    return [
        pltpu.VMEM((LANES * apart(cells), LANES), jnp.float32),
        pltpu.VMEM((lags, cells, LANES), jnp.float32),
        pltpu.SemaphoreType.DMA((4,)),
    ]


def early_spread(scale, cells, where, products):
    lags = 4 * cells + 1
    return pl.pallas_call(
        functools.partial(early_spread_body, scale, cells),
        in_specs=[SCALARS] + [WHOLE] * 2,
        out_specs=[WHOLE, pl.BlockSpec(memory_space=pl.ANY)],
        out_shape=[
            jax.ShapeDtypeStruct((apart(lags + 4 * cells) * cells, LANES), jnp.float32),
            pltpu.HBM((lags, cells, LANES), jnp.float32),
        ],
        scratch_shapes=spread_scratch(cells, 2 * cells + 1),
        compiler_params=params(),
        cost_estimate=pl.CostEstimate(flops=0, bytes_accessed=6 << 20, transcendentals=0),
        name="early_spread",
    )(where, *in_vmem(*products))


def late_spread_body(scale, cells, where_ref, kept_ref, came_ref, _, __, skewed_ref, image_ref, rows_ref, buffer_ref, sems):
    gather_rows(where_ref, cells, kept_ref, came_ref, rows_ref)
    spread_rows(where_ref, cells, (4, 5), scale, rows_ref, skewed_ref)
    write_lags((1 - where_ref[7]) * (2 * cells + 1), skewed_ref, image_ref, buffer_ref, sems)


def late_spread(scale, cells, where, products, skewed, image):
    return pl.pallas_call(
        functools.partial(late_spread_body, scale, cells),
        in_specs=[SCALARS] + [WHOLE] * 3 + [pl.BlockSpec(memory_space=pl.ANY)],
        out_specs=[WHOLE, pl.BlockSpec(memory_space=pl.ANY)],
        out_shape=[jax.ShapeDtypeStruct(skewed.shape, jnp.float32), pltpu.HBM(image.shape, jnp.float32)],
        input_output_aliases={3: 0, 4: 1},
        scratch_shapes=spread_scratch(cells, 2 * cells),
        compiler_params=params(),
        name="late_spread",
    )(where, *in_vmem(*products, skewed), image)[1]


def routed(source, receiver, scale):
    count = lax.axis_size("inline")
    cells = source.shape[1]
    own = lax.axis_index("inline")
    core, odd = own & 1, (own >> 1) & 1
    half = lax.axis_index("shot")

    def across(value):
        return lax.ppermute(value, "shot", [(0, 1), (1, 0)])

    def along_y(value):
        return lax.ppermute(value, "inline", [(index, index ^ 2) for index in range(count)])

    def along_z(value):
        pairs = [(index, index + (4, -4)[index // 2 % 2]) for index in range(count)]
        return lax.ppermute(value, "inline", [pair for pair in pairs if 0 <= pair[1] < count])

    def to_core(value):
        return lax.ppermute(value, "inline", [(index, index ^ 1) for index in range(count)])

    def across_to_core(value):
        pairs = [(2 * index + side, 2 * (index ^ 1) + 1 - side) for index in range(count) for side in range(2)]
        return lax.ppermute(value, ("inline", "shot"), pairs)

    def barrier(*values):
        return lax.optimization_barrier(values)

    receiver0, source0 = receiver, source
    side = 2 - 4 * odd
    where = jnp.stack([block + shift - core for shift in (0, side, -side) for block in (0, 1)] + [core, 1 - odd])
    where = where.astype(jnp.int32)
    kept, lent = turn(receiver0, half, core)
    y0 = along_y(kept)
    twin = to_core(lent)
    receiver_tied, *_ = barrier(receiver0, kept)
    there, there_twin = turn(receiver_tied, 1 - half, core)
    there_tied, *_ = barrier(there, twin)
    moved = across(there_tied)
    there_twin_tied, *_ = barrier(there_twin, twin)
    moved_twin = across_to_core(there_twin_tied)
    source_tied, *_ = barrier(source0, there)
    left, left_lent = turn(source_tied, half, core)
    source2_tied, *_ = barrier(source0, left)
    far, far_lent = turn(source2_tied, 1 - half, core)
    y1 = along_y(twin)
    y2 = along_y(moved)
    moved_twin_tied, *_ = barrier(moved_twin, y1)
    y3 = along_y(moved_twin_tied)
    y0_tied, *_ = barrier(y0, left)
    z0 = along_z(y0_tied)
    z1 = along_z(y1)
    left_lent_tied, *_ = barrier(left_lent, moved_twin)
    left_twin = to_core(left_lent_tied)
    far_tied, *_ = barrier(far, y1)
    right = across(far_tied)
    far_lent_tied, *_ = barrier(far_lent, y2)
    right_twin = across_to_core(far_lent_tied)
    y2_tied, *_ = barrier(y2, z0)
    z2 = along_z(y2_tied)
    left_twin_tied, *_ = barrier(left_twin, right)
    early = multiply(core, ([left], left_twin_tied), [(piece,) for piece in (kept, twin, y0, y1, z0, z1)])
    y3_tied, *_ = barrier(y3, z1)
    z3 = along_z(y3_tied)
    right_twin_tied, *_ = barrier(right_twin, z2)
    middle = multiply(core, ([right], right_twin_tied), ((moved,), (moved_twin,), (y2,), (y3,)), (early[0], early[2]))
    middle_came = to_core(middle[1])
    skewed, image = early_spread(scale, cells, where, (middle[0], middle_came))
    late = multiply(core, ([right], right_twin), ((z2,), (z3,)), (early[1], early[3]))
    late_came = to_core(late[1])
    return late_spread(scale, cells, where, (late[0], late_came), skewed, image)


def on_device(source, receiver):
    shots, cells, times, cross = source.shape
    groups, count = lax.axis_size("shot"), lax.axis_size("inline")
    scale = 1.0 / (times * shots * groups) ** 0.5
    fits = (
        groups == 2
        and count % 4 == 0
        and cross == 2 * LANES
        and shots * times == LANES
        and 4 * cells == LANES
        and times % ROWS == 0
    )
    return routed(source, receiver, scale) if fits else plain(source, receiver, scale)


def solution(mesh):
    placed = (P("shot", "inline", None, None), P("shot", "inline", None, None))
    return jax.shard_map(
        on_device, mesh=mesh, in_specs=placed, out_specs=P(None, "inline", "shot"), check_vma=False
    )
```
